32 devices in a mesh: groups: 2 (over y), mp: 4 (over x, core), dp: 4 (over z).
Axes of the slice: x: 2, y: 2, z: 4, core: 2. Of those that a mesh axis runs over, the one named last changes fastest.
Arguments:
- inputs: bfloat16 [1024, 6144], P(('groups', 'dp'), 'mp'), parts along dimension 0, may hold values from -6 to 6
- out_grad: bfloat16 [1024, 6144], P(('groups', 'dp'), 'mp'), parts along dimension 0, may hold values from -6 to 6
- up_weight: bfloat16 [4, 1536, 6144], P('mp'), may hold values from -0.15625 to 0.15625
- mix_weight: bfloat16 [4, 96, 256, 256], P(None, 'mp'), may hold values from -0.1875 to 0.1875
- output_factor_matrix: bfloat16 [4, 6144, 1536], P('mp'), may hold values from -0.078125 to 0.078125
- partner: int32 [2, 96], replicated, may hold values from 0 to 95, as said below
- local_perm: int32 [96], replicated, may hold values from 0 to 95, as said below
Outputs:
- outputs: bfloat16 [1024, 6144], P(('groups', 'dp'), 'mp'), parts along dimension 0
- input_grad: bfloat16 [1024, 6144], P(('groups', 'dp'), 'mp'), parts along dimension 0
- up_grad: float32 [8, 1536, 6144], P(('groups', 'mp'), None, 'dp'), parts along dimension 0
- mix_grad: float32 [8, 96, 256, 256], P('groups', 'mp', 'dp'), parts along dimension 0
- down_grad: float32 [8, 6144, 1536], P(('groups', 'mp'), 'dp'), parts along dimension 0
The draws below stay inside these ranges and needn't reach their ends.
There are 2 independent parts, one for each index of `groups`. The reference program is written for one: setup_inputs(seed, part) draws one part's arguments, and reference() takes and returns one part's arrays. A program takes and returns all parts, laid end to end along the dimension named above; an argument that names none is the same for every part. Nothing has to cross between parts.
Inputs may be any that keep to these rules, and one draw needn't show every extreme that they name: partner[l, b] // 24 equals b // 24 with bit l flipped; each row of partner is a permutation of the blocks. local_perm[b] // 24 equals b // 24; local_perm is a permutation of the blocks.
All inputs are finite; a program needn't handle non-finite values.
Results may differ from the reference program's by a relative error of at most 0.01.
Values may be sent and summed in bfloat16 or wider, within the bound.
No kernel may reach another device: no remote copies, remote signals or barrier semaphores. Data moves between devices by JAX's collectives and lax.ppermute only.
A program may use at most 320 MiB of HBM per device.

```python
import jax
import jax.numpy as jnp
from jax import lax

EMBED_DIMENSION = 6144
BLOCK_UNITS = 256
TOK_DEV = 128
LEVELS = 2
LV = 4
HIDDEN_BLOCKS = 96
BL = 24
GROUP_FEATURES = 1536
HG = 6144
TOKENS = 512
N_MP = 4
N_DP = 4


def shuffled(one_key):
    return jax.random.permutation(one_key, BL)


def draw_partner(key, part):
    key = jax.random.fold_in(key, 11)
    level_keys = jax.random.split(key, LEVELS * N_MP)
    slots = jax.vmap(shuffled)(level_keys).reshape(LEVELS, N_MP, BL)
    device_ids = jnp.arange(N_MP, dtype=jnp.int32)[None, :, None]
    level_ids = jnp.arange(LEVELS, dtype=jnp.int32)[:, None, None]
    target = jnp.bitwise_xor(device_ids, jnp.left_shift(jnp.ones_like(level_ids), level_ids))
    return (target * BL + slots).reshape(LEVELS, HIDDEN_BLOCKS).astype(jnp.int32)


def draw_local_perm(key, part):
    key = jax.random.fold_in(key, 23)
    group_keys = jax.random.split(key, N_MP)
    slots = jax.vmap(shuffled)(group_keys)
    device_ids = jnp.arange(N_MP, dtype=jnp.int32)[:, None]
    return (device_ids * BL + slots).reshape(HIDDEN_BLOCKS).astype(jnp.int32)


def block_levels(own_key, shape, cuts, smallest, largest):
    factor_of, own = 1.0, jax.random.fold_in(own_key, 6)
    for axis_at, shards_of in cuts:
        draws = jnp.exp(jax.random.uniform(jax.random.fold_in(own, axis_at), (shards_of,), jnp.float32, smallest / len(cuts), largest / len(cuts)))
        factor_of = factor_of * jnp.repeat(draws, shape[axis_at] // shards_of).reshape([-1 if axis == axis_at else 1 for axis in range(len(shape))])
    return factor_of


def noise(rng, shape, deviation, most, pieces=(), kind=jnp.bfloat16):
    drawn = jax.random.normal(rng, shape, jnp.float32) * deviation
    if len(pieces) > 0:
        drawn = block_levels(rng, shape, pieces, -0.22, 0.18) * drawn
    return jnp.clip(drawn, min=-most, max=most).astype(kind)


def setup_inputs(seed: int = 0, part: int = 0) -> dict:
    arg_keys = jax.random.split(jax.random.key(seed), 8)
    part_keys = jax.random.split(jax.random.fold_in(arg_keys[7], part), 8)
    return {
        "inputs": noise(part_keys[0], (TOKENS, EMBED_DIMENSION), 1.0, 6.0, ((0, 4), (1, 4))),
        "out_grad": noise(part_keys[1], (TOKENS, EMBED_DIMENSION), 1.0, 6.0, ((0, 4), (1, 4))),
        "up_weight": noise(arg_keys[2], (N_MP, GROUP_FEATURES, HG), GROUP_FEATURES ** -0.5, 0.15625, ((0, 4),)),
        "mix_weight": noise(arg_keys[3], (LV, HIDDEN_BLOCKS, BLOCK_UNITS, BLOCK_UNITS), (BLOCK_UNITS * LV) ** -0.5, 0.1875, ((1, 4),)),
        "output_factor_matrix": noise(arg_keys[4], (N_MP, HG, GROUP_FEATURES), HG ** -0.5, 0.078125, ((0, 4),)),
        "partner": draw_partner(jax.random.fold_in(arg_keys[7], 71), part),
        "local_perm": draw_local_perm(jax.random.fold_in(arg_keys[7], 71), part),
    }


def gelu_tanh(values):
    inner = 0.7978845608028654 * (values + 0.044715 * values * values * values)
    return 0.5 * values * (1.0 + jnp.tanh(inner))


def gelu_slope(values):
    inner = 0.7978845608028654 * (values + 0.044715 * values * values * values)
    tangent = jnp.tanh(inner)
    return 0.5 * (1.0 + tangent) + 0.5 * values * (1.0 - tangent * tangent) * 0.7978845608028654 * (1.0 + 3.0 * 0.044715 * values * values)


def reference(inputs, out_grad, up_weight, mix_weight, output_factor_matrix, partner, local_perm):
    sequence_entries = inputs.shape[0]
    input_wide = inputs.astype(jnp.float32).reshape(sequence_entries, N_MP, GROUP_FEATURES)
    hidden = jnp.einsum("tmd,mdh->tmh", input_wide, up_weight.astype(jnp.float32)).astype(jnp.bfloat16).reshape(sequence_entries, HIDDEN_BLOCKS, BLOCK_UNITS)
    block_ids = jnp.arange(HIDDEN_BLOCKS, dtype=jnp.int32)
    sources = jnp.concatenate([block_ids[None, :], local_perm[None, :].astype(jnp.int32), partner.astype(jnp.int32)], axis=0)
    hidden_wide = hidden.astype(jnp.float32)

    def forward_level(running, level_in):
        chosen, weight = level_in
        picked = jnp.take(hidden_wide, chosen, axis=1)
        return running + jnp.einsum("tbk,bkn->tbn", picked, weight.astype(jnp.float32)), None

    mixed_sum, unused = lax.scan(forward_level, jnp.zeros((sequence_entries, HIDDEN_BLOCKS, BLOCK_UNITS), jnp.float32), (sources, mix_weight))
    activated = gelu_tanh(mixed_sum).astype(jnp.bfloat16)
    nonlinear_output_full = activated.astype(jnp.float32).reshape(sequence_entries, N_MP, HG)
    butterfly_path_number = jnp.einsum("yje,jef->yjf", nonlinear_output_full, output_factor_matrix.astype(jnp.float32)).reshape(sequence_entries, EMBED_DIMENSION)
    outputs = (inputs.astype(jnp.float32) + butterfly_path_number).astype(jnp.bfloat16)

    gradient_wide = out_grad.astype(jnp.float32)
    activation_grad = jnp.einsum("afg,fjg->afj", gradient_wide.reshape(sequence_entries, N_MP, GROUP_FEATURES), output_factor_matrix.astype(jnp.float32)).reshape(sequence_entries, HIDDEN_BLOCKS, BLOCK_UNITS)
    delta_mixed = (activation_grad * gelu_slope(mixed_sum)).astype(jnp.bfloat16)
    delta_wide = delta_mixed.astype(jnp.float32)
    level_ids = jnp.arange(LV, dtype=jnp.int32)

    def backward_level(running, level_in):
        chosen, weight, level_num = level_in
        level_term = jnp.einsum("tbn,bkn->tbk", delta_wide, weight.astype(jnp.float32))
        rounded = lax.optimization_barrier(level_term.astype(jnp.bfloat16)).astype(jnp.float32)
        level_term = jnp.where(level_num >= 2, rounded, level_term)
        return running.at[:, chosen].add(level_term), None

    reverse_total, unused_back = lax.scan(backward_level, jnp.zeros((sequence_entries, HIDDEN_BLOCKS, BLOCK_UNITS), jnp.float32), (sources, mix_weight, level_ids))
    hidden_grad = reverse_total.astype(jnp.bfloat16)
    hidden_grad_wide = hidden_grad.astype(jnp.float32).reshape(sequence_entries, N_MP, HG)
    input_grad = (gradient_wide + jnp.einsum("tmh,mdh->tmd", hidden_grad_wide, up_weight.astype(jnp.float32)).reshape(sequence_entries, EMBED_DIMENSION)).astype(jnp.bfloat16)

    grad_scale = TOKENS ** -0.5

    def cluster_count(per_group):
        rounded = lax.optimization_barrier((per_group * grad_scale).astype(jnp.bfloat16))
        return jnp.sum(rounded.astype(jnp.float32), axis=0)

    up_grad = cluster_count(jnp.einsum("gtmd,gtmh->gmdh", input_wide.reshape(N_DP, TOK_DEV, N_MP, GROUP_FEATURES), hidden_grad_wide.reshape(N_DP, TOK_DEV, N_MP, HG)))
    down_grad = cluster_count(jnp.einsum("gtmh,gtmd->gmhd", nonlinear_output_full.reshape(N_DP, TOK_DEV, N_MP, HG), gradient_wide.reshape(N_DP, TOK_DEV, N_MP, GROUP_FEATURES)))
    delta_groups = delta_wide.reshape(N_DP, TOK_DEV, HIDDEN_BLOCKS, BLOCK_UNITS)

    def grad_level(chosen):
        picked = jnp.take(hidden_wide, chosen, axis=1).reshape(N_DP, TOK_DEV, HIDDEN_BLOCKS, BLOCK_UNITS)
        return cluster_count(jnp.einsum("gtbk,gtbn->gbkn", picked, delta_groups))

    mix_grad = lax.map(grad_level, sources)
    return (outputs, input_grad, up_grad, mix_grad, down_grad)
```

```python
import functools

import jax
import jax.numpy as jnp
from jax import lax
from jax.experimental import pallas as pl
from jax.experimental.pallas import tpu as pltpu
from jax.sharding import PartitionSpec as P

F32 = jnp.float32
BF16 = jnp.bfloat16
VMEM_BYTES = 56 * 1024 * 1024


def from_partner(value, axis, apart):
    mask = 2**apart
    pairs = [(source, source ^ mask) for source in range(lax.axis_size(axis))]
    return lax.ppermute(value, axis, pairs)


def rotated(value, axis, shift):
    size = lax.axis_size(axis)
    return lax.ppermute(value, axis, [(i, (i + shift) % size) for i in range(size)])


def gelu_tanh(values):
    inner = 0.7978845608028654 * (values + 0.044715 * values * values * values)
    return 0.5 * values * (1.0 + jnp.tanh(inner))


def gelu_slope(values):
    inner = 0.7978845608028654 * (values + 0.044715 * values * values * values)
    tangent = jnp.tanh(inner)
    return 0.5 * (1.0 + tangent) + 0.5 * values * (1.0 - tangent * tangent) * 0.7978845608028654 * (
        1.0 + 3.0 * 0.044715 * values * values
    )


def dot(a, b):
    return jnp.dot(a, b, preferred_element_type=F32)


def dot_nt(a, b):
    return lax.dot_general(a, b, (((1,), (1,)), ((), ())), preferred_element_type=F32)


def dot_tn(a, b):
    return lax.dot_general(a, b, (((0,), (0,)), ((), ())), preferred_element_type=F32)


def params():
    return pltpu.CompilerParams(vmem_limit_bytes=VMEM_BYTES)


def chunk_of(block_count, most):
    return max(c for c in range(1, most + 1) if block_count % c == 0)


def lanes(index, size):
    return pl.ds(pl.multiple_of(index * size, size), size)


def whole(shape):
    return pl.BlockSpec(shape, lambda i, *_: (0,) * len(shape))


def weight_specs(levels, chunk, size):
    return [
        pl.BlockSpec((1, chunk, size, size), functools.partial(lambda lv, i, *_: (lv, i, 0, 0), lv))
        for lv in levels
    ]


def mixed_near(sources, which, index, levels, mix_weight):
    rows, width = sources[0].shape
    blocks, size = mix_weight.shape[1], mix_weight.shape[2]
    chunk = chunk_of(blocks, 4)
    count = len(levels)

    def kernel(index_ref, *refs):
        source_refs, weight_refs, out_ref = refs[: len(sources)], refs[len(sources) : -1], refs[-1]
        step = pl.program_id(0)
        for c in range(chunk):
            total = None
            for k in range(count):
                picked = source_refs[which[k]][:, lanes(index_ref[k, step * chunk + c], size)]
                term = dot(picked, weight_refs[k][0, c])
                total = term if total is None else total + term
            out_ref[:, c * size : (c + 1) * size] = total

    return pl.pallas_call(
        kernel,
        grid_spec=pltpu.PrefetchScalarGridSpec(
            num_scalar_prefetch=1,
            grid=(blocks // chunk,),
            in_specs=[whole((rows, width)) for _ in sources] + weight_specs(levels, chunk, size),
            out_specs=pl.BlockSpec((rows, chunk * size), lambda i, *_: (0, i)),
        ),
        out_shape=jax.ShapeDtypeStruct((rows, width), F32),
        compiler_params=params(),
        name="mixed_near",
    )(index, *sources, *([mix_weight] * count))


def mixed_last(source, index, level, mix_weight, near, act_grad):
    rows, width = source.shape
    blocks, size = mix_weight.shape[1], mix_weight.shape[2]
    chunk = chunk_of(blocks, 4)

    def kernel(index_ref, source_ref, weight_ref, near_ref, grad_ref, mixed_ref, act_ref, delta_ref):
        step = pl.program_id(0)
        for c in range(chunk):
            here = slice(c * size, (c + 1) * size)
            picked = source_ref[:, lanes(index_ref[step * chunk + c], size)]
            total = near_ref[:, here] + dot(picked, weight_ref[0, c])
            mixed_ref[:, here] = total.astype(BF16)
            act_ref[:, here] = gelu_tanh(total).astype(BF16)
            delta_ref[:, here] = (grad_ref[:, here] * gelu_slope(total)).astype(BF16)

    columns = pl.BlockSpec((rows, chunk * size), lambda i, *_: (0, i))
    return pl.pallas_call(
        kernel,
        grid_spec=pltpu.PrefetchScalarGridSpec(
            num_scalar_prefetch=1,
            grid=(blocks // chunk,),
            in_specs=[whole((rows, width))] + weight_specs([level], chunk, size) + [columns, columns],
            out_specs=[columns] * 3,
        ),
        out_shape=[jax.ShapeDtypeStruct((rows, width), BF16)] * 3,
        compiler_params=params(),
        name="mixed_last",
    )(index, source, mix_weight, near, act_grad)


def far_terms(delta, targets, levels, mix_weight):
    rows, width = delta.shape
    blocks, size = mix_weight.shape[1], mix_weight.shape[2]
    chunk = chunk_of(blocks, 4)
    count = len(levels)

    def kernel(target_ref, delta_ref, *refs):
        step = pl.program_id(0)
        for c in range(chunk):
            here = delta_ref[:, c * size : (c + 1) * size]
            for k in range(count):
                place = lanes(target_ref[k, step * chunk + c], size)
                refs[count + k][:, place] = dot_nt(here, refs[k][0, c]).astype(BF16)

    return pl.pallas_call(
        kernel,
        grid_spec=pltpu.PrefetchScalarGridSpec(
            num_scalar_prefetch=1,
            grid=(blocks // chunk,),
            in_specs=[pl.BlockSpec((rows, chunk * size), lambda i, *_: (0, i))]
            + weight_specs(levels, chunk, size),
            out_specs=[whole((rows, width))] * count,
        ),
        out_shape=[jax.ShapeDtypeStruct((rows, width), BF16)] * count,
        compiler_params=params(),
        name="far_terms",
    )(targets, delta, *([mix_weight] * count))


def near_terms(delta, perm, mix_weight):
    rows, width = delta.shape
    blocks, size = mix_weight.shape[1], mix_weight.shape[2]
    chunk = chunk_of(blocks, 4)

    def kernel(perm_ref, delta_ref, own_ref, perm_weight_ref, out_ref):
        step = pl.program_id(0)

        @pl.when(step == 0)
        def _():
            out_ref[...] = jnp.zeros_like(out_ref)

        for c in range(chunk):
            here = delta_ref[:, c * size : (c + 1) * size]
            out_ref[:, lanes(step * chunk + c, size)] += dot_nt(here, own_ref[0, c])
            out_ref[:, lanes(perm_ref[step * chunk + c], size)] += dot_nt(here, perm_weight_ref[0, c])

    return pl.pallas_call(
        kernel,
        grid_spec=pltpu.PrefetchScalarGridSpec(
            num_scalar_prefetch=1,
            grid=(blocks // chunk,),
            in_specs=[pl.BlockSpec((rows, chunk * size), lambda i, *_: (0, i))]
            + weight_specs([0, 1], chunk, size),
            out_specs=whole((rows, width)),
        ),
        out_shape=jax.ShapeDtypeStruct((rows, width), F32),
        compiler_params=params(),
        name="near_terms",
    )(perm, delta, mix_weight, mix_weight)


def mix_gradient(mixed_all, out_grad_all, down, sources, which, index, scale):
    tokens, width = mixed_all.shape
    blocks, part, _ = sources[0].shape
    size = width // blocks
    chunk = chunk_of(blocks, 2)
    features = out_grad_all.shape[1]
    count = len(which)

    def kernel(index_ref, mixed_ref, grad_ref, down_ref, *refs):
        source_refs, out_ref = refs[:-1], refs[-1]
        step = pl.program_id(0)
        for c in range(chunk):
            here = slice(c * size, (c + 1) * size)
            act_grad = dot_nt(grad_ref[...], down_ref[here, :])
            slope = gelu_slope(mixed_ref[:, here].astype(F32))
            delta = (act_grad * slope).astype(BF16)
            picked = jnp.concatenate(
                [source_refs[which[k]][index_ref[k, step * chunk + c]] for k in range(count)], axis=0
            )
            result = dot(picked, delta) * scale
            for k in range(count):
                out_ref[k, c] = result[k * part : (k + 1) * part]

    return pl.pallas_call(
        kernel,
        grid_spec=pltpu.PrefetchScalarGridSpec(
            num_scalar_prefetch=1,
            grid=(blocks // chunk,),
            in_specs=[
                pl.BlockSpec((tokens, chunk * size), lambda i, *_: (0, i)),
                whole((tokens, features)),
                pl.BlockSpec((chunk * size, features), lambda i, *_: (i, 0)),
            ]
            + [whole((blocks, part, tokens)) for _ in sources],
            out_specs=pl.BlockSpec((count, chunk, part, size), lambda i, *_: (0, i, 0, 0)),
        ),
        out_shape=jax.ShapeDtypeStruct((count, blocks, part, size), F32),
        compiler_params=params(),
        name="mix_gradient",
    )(index, mixed_all, out_grad_all, down, *sources)


def gathered(value, axis):
    size = lax.axis_size(axis)
    me = lax.axis_index(axis)
    pieces = jnp.stack([value] + [rotated(value, axis, s) for s in range(1, size)])
    order = (me - jnp.arange(size, dtype=jnp.int32)) % size
    return jnp.take(pieces, order, axis=0, mode="clip").reshape(size * value.shape[0], value.shape[1])


def exchanged(value, axis):
    size = lax.axis_size(axis)
    me = lax.axis_index(axis)
    rows = value.shape[0]
    share = value.shape[1] // size
    pieces = []
    for s in range(size):
        piece = lax.dynamic_slice_in_dim(value, ((me + s) % size) * share, share, 1)
        pieces.append(rotated(piece, axis, s) if s else piece)
    order = (me - jnp.arange(size, dtype=jnp.int32)) % size
    return jnp.take(jnp.stack(pieces), order, axis=0, mode="clip").reshape(size * rows, share)


def body(inputs, out_grad, up_weight, mix_weight, output_factor_matrix, partner, local_perm):
    rows = inputs.shape[0]
    blocks, size = mix_weight.shape[1], mix_weight.shape[2]
    levels = partner.shape[0]
    up, down = up_weight[0], output_factor_matrix[0]
    width = up.shape[1]
    runs = lax.axis_size("dp")
    me, run = lax.axis_index("mp"), lax.axis_index("dp")
    base = me * blocks
    scale = (rows * runs) ** (-0.5)
    perm_here = lax.dynamic_slice_in_dim(local_perm, base, blocks, 0) - base
    far_here = lax.dynamic_slice_in_dim(partner, base, blocks, 1)
    far_base = jnp.stack([jnp.bitwise_xor(me, 1 << lv) * blocks for lv in range(levels)])
    far_index = far_here - far_base[:, None]
    index = jnp.concatenate(
        [jnp.arange(blocks, dtype=jnp.int32)[None], perm_here[None], far_index], axis=0
    )
    which = [0, 0] + list(range(1, levels + 1))
    last = levels + 1

    hidden = dot(inputs, up).astype(BF16)
    received = [from_partner(hidden, "mp", lv) for lv in range(levels)]
    inputs_all = gathered(inputs, "dp")
    out_grad_all = gathered(out_grad, "dp")
    act_grad = dot_nt(out_grad, down)
    near = mixed_near(
        [hidden] + received[:-1], which[:-1], index[:-1], list(range(last)), mix_weight
    )
    mixed, activated, delta = mixed_last(
        received[-1], index[-1], last, mix_weight, near, act_grad
    )
    mixed_all = lax.all_gather(mixed, "dp", axis=0, tiled=True)

    far = far_terms(delta, far_index, list(range(2, levels + 2)), mix_weight)
    far_received = [from_partner(far[lv], "mp", lv) for lv in range(levels)]
    back = near_terms(delta, perm_here, mix_weight)

    hidden_part = (
        lax.dot_general(up, inputs_all, (((0,), (1,)), ((), ())), preferred_element_type=F32)
        .astype(BF16)
        .reshape(blocks, size, runs * rows)
    )
    part = size // runs
    hidden_part = lax.dynamic_slice_in_dim(hidden_part, run * part, part, 1)
    part_received = [from_partner(hidden_part, "mp", lv) for lv in range(levels)]

    outputs = (inputs.astype(F32) + dot(activated, down)).astype(BF16)
    for term in far_received:
        back = back + term.astype(F32)
    hidden_grad = back.astype(BF16)
    hidden_grad_part = exchanged(hidden_grad, "dp")
    input_grad = (out_grad.astype(F32) + dot_nt(hidden_grad, up)).astype(BF16)
    up_grad = dot_tn(inputs_all, hidden_grad_part) * scale

    mix_grad = mix_gradient(
        mixed_all, out_grad_all, down, [hidden_part] + part_received, which, index, scale
    )
    share = width // runs
    mixed_part = lax.dynamic_slice_in_dim(mixed_all, run * share, share, 1)
    activated_part = gelu_tanh(mixed_part.astype(F32)).astype(BF16)
    down_grad = dot_tn(activated_part, out_grad_all) * scale
    return (outputs, input_grad, up_grad[None], mix_grad, down_grad[None])


def solution(mesh):
    return jax.shard_map(
        body,
        mesh=mesh,
        in_specs=(
            P(("groups", "dp"), "mp"),
            P(("groups", "dp"), "mp"),
            P("mp", None, None),
            P(None, "mp", None, None),
            P("mp", None, None),
            P(),
            P(),
        ),
        out_specs=(
            P(("groups", "dp"), "mp"),
            P(("groups", "dp"), "mp"),
            P(("groups", "mp"), None, "dp"),
            P("groups", "mp", "dp", None),
            P(("groups", "mp"), "dp", None),
        ),
        check_vma=False,
    )
```

```python
import functools
import math

import jax
import jax.numpy as jnp
from jax import lax
from jax.experimental import pallas as pl
from jax.experimental.pallas import tpu as pltpu
from jax.sharding import PartitionSpec as P

F32 = jnp.float32
BF16 = jnp.bfloat16
VMEM_BYTES = 56 * 1024 * 1024
ANY = pl.BlockSpec(memory_space=pl.ANY)


def from_partner(value, axis, apart):
    mask = 2**apart
    pairs = [(source, source ^ mask) for source in range(lax.axis_size(axis))]
    return lax.ppermute(value, axis, pairs)


def rotated(value, axis, shift):
    size = lax.axis_size(axis)
    return lax.ppermute(value, axis, [(i, (i + shift) % size) for i in range(size)])


def gelu_tanh(values):
    inner = 0.7978845608028654 * (values + 0.044715 * values * values * values)
    return 0.5 * values * (1.0 + jnp.tanh(inner))


def gelu_slope(values):
    inner = 0.7978845608028654 * (values + 0.044715 * values * values * values)
    tangent = jnp.tanh(inner)
    return 0.5 * (1.0 + tangent) + 0.5 * values * (1.0 - tangent * tangent) * 0.7978845608028654 * (
        1.0 + 3.0 * 0.044715 * values * values
    )


def dot(a, b):
    return jnp.dot(a, b, preferred_element_type=F32)


def dot_nt(a, b):
    return lax.dot_general(a, b, (((1,), (1,)), ((), ())), preferred_element_type=F32)


def dot_tn(a, b):
    return lax.dot_general(a, b, (((0,), (0,)), ((), ())), preferred_element_type=F32)


def params():
    return pltpu.CompilerParams(vmem_limit_bytes=VMEM_BYTES)


def cost(*arrays):
    moved = sum(math.prod(a.shape) * a.dtype.itemsize for a in arrays)
    return pl.CostEstimate(flops=0, bytes_accessed=int(2.2 * moved), transcendentals=0)


def level_shape(mix_weight):
    return jax.ShapeDtypeStruct(mix_weight.shape[1:], mix_weight.dtype)


def chunk_of(block_count, most):
    return max(c for c in range(1, most + 1) if block_count % c == 0)


def lanes(index, size):
    return pl.ds(pl.multiple_of(index * size, size), size)


def whole(shape):
    return pl.BlockSpec(shape, lambda i, *_: (0,) * len(shape))


def column_half(tokens, features, half):
    return pl.BlockSpec((tokens, features), lambda i, *_: (0, half))


def weight_specs(levels, chunk, size):
    return [
        pl.BlockSpec((1, chunk, size, size), functools.partial(lambda lv, i, *_: (lv, i, 0, 0), lv))
        for lv in levels
    ]


def mixed_near(sources, which, index, levels, mix_weight, after=()):
    rows, width = sources[0].shape
    blocks, size = mix_weight.shape[1], mix_weight.shape[2]
    chunk = chunk_of(blocks, 4)
    count = len(levels)
    near_shape = jax.ShapeDtypeStruct((rows, width), F32)

    def kernel(index_ref, *refs):
        source_refs, weight_refs, out_ref = refs[: len(sources)], refs[len(sources) :], refs[-1]
        step = pl.program_id(0)
        for c in range(chunk):
            total = None
            for k in range(count):
                picked = source_refs[which[k]][:, lanes(index_ref[k, step * chunk + c], size)]
                term = dot(picked, weight_refs[k][0, c])
                total = term if total is None else total + term
            out_ref[:, c * size : (c + 1) * size] = total

    return pl.pallas_call(
        kernel,
        grid_spec=pltpu.PrefetchScalarGridSpec(
            num_scalar_prefetch=1,
            grid=(blocks // chunk,),
            in_specs=[whole((rows, width)) for _ in sources]
            + weight_specs(levels, chunk, size)
            + [ANY] * len(after),
            out_specs=pl.BlockSpec((rows, chunk * size), lambda i, *_: (0, i)),
        ),
        out_shape=near_shape,
        compiler_params=params(),
        name="mixed_near",
        cost_estimate=cost(*sources, *[level_shape(mix_weight)] * count, near_shape),
    )(index, *sources, *([mix_weight] * count), *after)


def mixed_last(source, index, level, mix_weight, near, act_grad, kept, after=()):
    rows, width = source.shape
    blocks, size = mix_weight.shape[1], mix_weight.shape[2]
    chunk = chunk_of(math.gcd(blocks, kept), 4)

    def kernel(index_ref, source_ref, weight_ref, near_ref, grad_ref, *refs):
        mixed_ref, act_ref, delta_ref = refs[-3:]
        step = pl.program_id(0)
        for c in range(chunk):
            here = slice(c * size, (c + 1) * size)
            picked = source_ref[:, lanes(index_ref[step * chunk + c], size)]
            total = near_ref[:, here] + dot(picked, weight_ref[0, c])

            @pl.when(step < kept // chunk)
            def _(total=total, here=here):
                mixed_ref[:, here] = total.astype(BF16)

            act_ref[:, here] = gelu_tanh(total).astype(BF16)
            delta_ref[:, here] = (grad_ref[:, here] * gelu_slope(total)).astype(BF16)

    columns = pl.BlockSpec((rows, chunk * size), lambda i, *_: (0, i))
    return pl.pallas_call(
        kernel,
        grid_spec=pltpu.PrefetchScalarGridSpec(
            num_scalar_prefetch=1,
            grid=(blocks // chunk,),
            in_specs=[whole((rows, width))] + weight_specs([level], chunk, size)
            + [columns, columns]
            + [ANY] * len(after),
            out_specs=[
                pl.BlockSpec((rows, chunk * size), lambda i, *_: (0, jnp.minimum(i, kept // chunk - 1))),
                columns,
                columns,
            ],
        ),
        out_shape=[jax.ShapeDtypeStruct((rows, kept * size), BF16)]
        + [jax.ShapeDtypeStruct((rows, width), BF16)] * 2,
        compiler_params=params(),
        name="mixed_last",
        cost_estimate=cost(source, level_shape(mix_weight), near, act_grad, source, source),
    )(index, source, mix_weight, near, act_grad, *after)


def far_terms(delta, targets, levels, mix_weight):
    rows, width = delta.shape
    blocks, size = mix_weight.shape[1], mix_weight.shape[2]
    chunk = chunk_of(blocks, 4)
    count = len(levels)

    def kernel(target_ref, delta_ref, *refs):
        step = pl.program_id(0)
        for c in range(chunk):
            here = delta_ref[:, c * size : (c + 1) * size]
            for k in range(count):
                place = lanes(target_ref[k, step * chunk + c], size)
                refs[count + k][:, place] = dot_nt(here, refs[k][0, c]).astype(BF16)

    return pl.pallas_call(
        kernel,
        grid_spec=pltpu.PrefetchScalarGridSpec(
            num_scalar_prefetch=1,
            grid=(blocks // chunk,),
            in_specs=[pl.BlockSpec((rows, chunk * size), lambda i, *_: (0, i))]
            + weight_specs(levels, chunk, size),
            out_specs=[whole((rows, width))] * count,
        ),
        out_shape=[jax.ShapeDtypeStruct((rows, width), BF16)] * count,
        compiler_params=params(),
        name="far_terms",
        cost_estimate=cost(delta, *[level_shape(mix_weight), delta] * count),
    )(targets, delta, *([mix_weight] * count))


def near_terms(delta, perm, mix_weight, after=()):
    rows, width = delta.shape
    blocks, size = mix_weight.shape[1], mix_weight.shape[2]
    chunk = chunk_of(blocks, 4)

    def kernel(perm_ref, delta_ref, own_ref, perm_weight_ref, *refs):
        out_ref = refs[-1]
        step = pl.program_id(0)

        @pl.when(step == 0)
        def _():
            out_ref[...] = jnp.zeros_like(out_ref)

        for c in range(chunk):
            here = delta_ref[:, c * size : (c + 1) * size]
            out_ref[:, lanes(step * chunk + c, size)] += dot_nt(here, own_ref[0, c])
            out_ref[:, lanes(perm_ref[step * chunk + c], size)] += dot_nt(here, perm_weight_ref[0, c])

    return pl.pallas_call(
        kernel,
        grid_spec=pltpu.PrefetchScalarGridSpec(
            num_scalar_prefetch=1,
            grid=(blocks // chunk,),
            in_specs=[pl.BlockSpec((rows, chunk * size), lambda i, *_: (0, i))]
            + weight_specs([0, 1], chunk, size)
            + [ANY] * len(after),
            out_specs=whole((rows, width)),
        ),
        out_shape=jax.ShapeDtypeStruct((rows, width), F32),
        compiler_params=params(),
        name="near_terms",
        cost_estimate=cost(delta, delta, delta, *[level_shape(mix_weight)] * 2),
    )(perm, delta, mix_weight, mix_weight, *after)


def dense(left, right, out_type, right_transposed=False, after=()):
    rows, depth = left.shape
    width = right.shape[0] if right_transposed else right.shape[1]
    step = chunk_of(width // 128, 12) * 128
    out_shape = jax.ShapeDtypeStruct((rows, width), out_type)
    if right_transposed:
        right_spec = pl.BlockSpec((step, depth), lambda i: (i, 0))
    else:
        right_spec = pl.BlockSpec((depth, step), lambda i: (0, i))

    def kernel(left_ref, right_ref, *refs):
        product = (dot_nt if right_transposed else dot)(left_ref[...], right_ref[...])
        refs[-1][...] = product.astype(out_type)

    return pl.pallas_call(
        kernel,
        grid=(width // step,),
        in_specs=[whole((rows, depth)), right_spec] + [ANY] * len(after),
        out_specs=pl.BlockSpec((rows, step), lambda i: (0, i)),
        out_shape=out_shape,
        compiler_params=params(),
        name="dense_nt" if right_transposed else "dense",
        cost_estimate=cost(left, right, out_shape),
    )(left, right, *after)


def dense_added(left, right, base, right_transposed=False, after=()):
    rows, depth = left.shape
    width = base.shape[1]
    step = chunk_of(depth // 128, 12) * 128
    if right_transposed:
        right_spec = pl.BlockSpec((width, step), lambda i: (0, i))
    else:
        right_spec = pl.BlockSpec((step, width), lambda i: (i, 0))

    def kernel(left_ref, right_ref, base_ref, *refs):
        out_ref, total_ref = refs[-2], refs[-1]
        here = pl.program_id(0)

        @pl.when(here == 0)
        def _():
            total_ref[...] = base_ref[...].astype(F32)

        total_ref[...] += (dot_nt if right_transposed else dot)(left_ref[...], right_ref[...])

        @pl.when(here == depth // step - 1)
        def _():
            out_ref[...] = total_ref[...].astype(out_ref.dtype)

    return pl.pallas_call(
        kernel,
        grid=(depth // step,),
        in_specs=[pl.BlockSpec((rows, step), lambda i: (0, i)), right_spec, whole(base.shape)]
        + [ANY] * len(after),
        out_specs=whole(base.shape),
        out_shape=jax.ShapeDtypeStruct(base.shape, base.dtype),
        scratch_shapes=[pltpu.VMEM(base.shape, F32)],
        compiler_params=params(),
        name="added_nt" if right_transposed else "added",
        cost_estimate=cost(left, right, base),
    )(left, right, base, *after)


def hidden_rows(up, gathered, run, places, blocks, kept, part, after=()):
    depth, width = up.shape
    tokens = gathered.shape[0]
    size = width // blocks
    chunk = chunk_of(blocks, 4)
    levels = places.shape[0]
    again = blocks - kept
    sent = jax.ShapeDtypeStruct((again * size + kept * part, tokens), BF16)

    def kernel(run_ref, place_ref, up_ref, inputs_ref, *refs):
        whole_ref, out_ref = refs[-3 - levels : -1 - levels]
        sent_refs, full_ref = refs[-1 - levels : -1], refs[-1]
        full_ref[...] = lax.dot_general(
            up_ref[...], inputs_ref[...], (((0,), (1,)), ((), ())), preferred_element_type=F32
        )
        for c in range(chunk):
            first = pl.multiple_of(run_ref[0] * part, part) + c * size
            whole_ref[c] = full_ref[c * size : (c + 1) * size].astype(BF16)
            out_ref[c] = full_ref[pl.ds(first, part), :].astype(BF16)
            for lv in range(levels):
                place = place_ref[lv, pl.program_id(0) * chunk + c]

                if again:

                    @pl.when(place >= kept)
                    def _(place=place, lv=lv, c=c):
                        there = pl.multiple_of((place - kept) * size, size)
                        sent_refs[lv][pl.ds(there, size), :] = whole_ref[c]

                @pl.when(place < kept)
                def _(place=place, lv=lv, c=c):
                    there = pl.multiple_of(again * size + place * part, part)
                    sent_refs[lv][pl.ds(there, part), :] = out_ref[c]

    return pl.pallas_call(
        kernel,
        grid_spec=pltpu.PrefetchScalarGridSpec(
            num_scalar_prefetch=2,
            grid=(blocks // chunk,),
            in_specs=[
                pl.BlockSpec((depth, chunk * size), lambda i, *_: (0, i)),
                column_half(tokens, depth, 0),
            ]
            + [ANY] * len(after),
            out_specs=[
                pl.BlockSpec((chunk, size, tokens), lambda i, *_: (i, 0, 0)),
                pl.BlockSpec((chunk, part, tokens), lambda i, *_: (i, 0, 0)),
            ]
            + [whole(sent.shape)] * levels,
            scratch_shapes=[pltpu.VMEM((chunk * size, tokens), F32)],
        ),
        out_shape=[
            jax.ShapeDtypeStruct((blocks, size, tokens), BF16),
            jax.ShapeDtypeStruct((blocks, part, tokens), BF16),
        ]
        + [sent] * levels,
        compiler_params=params(),
        name="hidden_rows",
        cost_estimate=cost(up, jax.ShapeDtypeStruct((blocks, size, tokens), BF16)),
    )(run, places, up, gathered, *after)


def down_pass(activated, down, base, gathered, kept, after=()):
    rows, width = activated.shape
    features = down.shape[1]
    tokens = gathered.shape[0]
    step = chunk_of(math.gcd(width, kept) // 128, 8) * 128

    def kernel(act_ref, down_ref, base_ref, all_ref, *refs):
        out_ref, grad_ref, total_ref = refs[-3:]
        here = pl.program_id(0)

        @pl.when(here == 0)
        def _():
            total_ref[...] = base_ref[...].astype(F32)

        total_ref[...] += dot(act_ref[...], down_ref[...])

        @pl.when(here < kept // step)
        def _():
            grad_ref[...] = dot_nt(all_ref[...], down_ref[...])

        @pl.when(here == width // step - 1)
        def _():
            out_ref[...] = total_ref[...].astype(BF16)

    return pl.pallas_call(
        kernel,
        grid=(width // step,),
        in_specs=[
            pl.BlockSpec((rows, step), lambda i: (0, i)),
            pl.BlockSpec((step, features), lambda i: (i, 0)),
            whole((rows, features)),
            column_half(tokens, features, 1),
        ]
        + [ANY] * len(after),
        out_specs=[
            whole((rows, features)),
            pl.BlockSpec((tokens, step), lambda i: (0, jnp.minimum(i, kept // step - 1))),
        ],
        out_shape=[
            jax.ShapeDtypeStruct((rows, features), BF16),
            jax.ShapeDtypeStruct((tokens, kept), F32),
        ],
        scratch_shapes=[pltpu.VMEM((rows, features), F32)],
        compiler_params=params(),
        name="down_pass",
        cost_estimate=cost(activated, down, jax.ShapeDtypeStruct((tokens, kept), F32)),
    )(activated, down, base, gathered, *after)


def mix_gradient(mixed_all, act_grad_all, hidden_part, received, perm, scale, made=None):
    tokens, width = mixed_all.shape
    blocks, part, _ = hidden_part.shape
    size = part * lax.axis_size("dp")
    kept = width // size
    chunk = chunk_of(kept, 4)
    count = 2 + len(received)
    given = pl.BlockSpec(
        (kept * part, tokens), lambda i, *_: ((blocks - kept) * size // (kept * part), 0)
    )

    def kernel(perm_ref, mixed_ref, grad_ref, part_ref, *refs):
        given_refs, out_ref = refs[: len(received)], refs[-1]
        step = pl.program_id(0)
        for c in range(chunk):
            here = slice(c * size, (c + 1) * size)
            block = step * chunk + c
            slope = gelu_slope(mixed_ref[:, here].astype(F32))
            delta = (grad_ref[:, here] * slope).astype(BF16)
            rows = pl.ds(pl.multiple_of(block * part, part), part)
            picked = jnp.concatenate(
                [part_ref[block], part_ref[perm_ref[block]]] + [ref[rows, :] for ref in given_refs],
                axis=0,
            )
            result = dot(picked, delta) * scale
            for k in range(count):
                out_ref[k, c] = result[k * part : (k + 1) * part]

    columns = pl.BlockSpec((tokens, chunk * size), lambda i, *_: (0, i))
    return pl.pallas_call(
        kernel,
        grid_spec=pltpu.PrefetchScalarGridSpec(
            num_scalar_prefetch=1,
            grid=(kept // chunk,),
            in_specs=[columns, columns, whole(hidden_part.shape)]
            + [given] * len(received)
            + ([] if made is None else [ANY]),
            out_specs=pl.BlockSpec((count, chunk, part, size), lambda i, *_: (0, i, 0, 0)),
        ),
        out_shape=jax.ShapeDtypeStruct((count, blocks, part, size), F32),
        input_output_aliases={} if made is None else {4 + len(received): 0},
        compiler_params=params(),
        name="mix_gradient",
        cost_estimate=cost(mixed_all, act_grad_all),
    )(perm, mixed_all, act_grad_all, hidden_part, *received, *([] if made is None else [made]))


def recomputed(hidden_all, received, again, index, down, gathered, run, mix_weight, scale, after=()):
    blocks, size, tokens = hidden_all.shape
    count = mix_weight.shape[0]
    kept = blocks - again
    part = size // lax.axis_size("dp")
    features = down.shape[1]

    def kernel(index_ref, run_ref, *refs):
        source_refs, weight_refs = refs[:count], refs[count : 2 * count]
        down_ref, grad_ref = refs[2 * count : 2 * count + 2]
        out_ref, act_ref = refs[-2:]
        mixed = None
        sources = [ref.at[0] if k < 2 else ref for k, ref in enumerate(source_refs)]
        for k in range(count):
            term = dot_tn(weight_refs[k][0, 0], sources[k][...])
            mixed = term if mixed is None else mixed + term
        act_ref[0] = gelu_tanh(mixed).astype(BF16)
        act_grad = dot_nt(down_ref[...], grad_ref[...])
        delta = (act_grad * gelu_slope(mixed)).astype(BF16)
        first = pl.multiple_of(run_ref[0] * part, part)
        picked = jnp.concatenate(
            [sources[k][pl.ds(first, part), :] for k in range(count)], axis=0
        )
        result = dot_nt(picked, delta) * scale
        for k in range(count):
            out_ref[k, 0] = result[k * part : (k + 1) * part]

    source_specs = [
        pl.BlockSpec((1, size, tokens), lambda i, *_: (kept + i, 0, 0)),
        pl.BlockSpec((1, size, tokens), lambda i, index, run: (index[kept + i], 0, 0)),
    ] + [pl.BlockSpec((size, tokens), lambda i, *_: (i, 0))] * len(received)
    level_specs = [
        pl.BlockSpec(
            (1, 1, size, size), functools.partial(lambda k, i, *_: (k, kept + i, 0, 0), k)
        )
        for k in range(count)
    ]
    return pl.pallas_call(
        kernel,
        grid_spec=pltpu.PrefetchScalarGridSpec(
            num_scalar_prefetch=2,
            grid=(again,),
            in_specs=source_specs
            + level_specs
            + [
                pl.BlockSpec((size, features), lambda i, *_: (kept + i, 0)),
                column_half(tokens, features, 1),
            ]
            + [ANY] * len(after),
            out_specs=[
                pl.BlockSpec((count, 1, part, size), lambda i, *_: (0, kept + i, 0, 0)),
                pl.BlockSpec((1, size, tokens), lambda i, *_: (i, 0, 0)),
            ],
        ),
        out_shape=[
            jax.ShapeDtypeStruct((count, blocks, part, size), F32),
            jax.ShapeDtypeStruct((again, size, tokens), BF16),
        ],
        compiler_params=params(),
        name="recomputed",
        cost_estimate=cost(*received, *received, gathered, level_shape(mix_weight)),
    )(
        index, run, hidden_all, hidden_all, *received, *([mix_weight] * count), down, gathered,
        *after,
    )


def up_gradient(gathered, height, pieces, run_rows, scale, after=()):
    tokens = gathered.shape[0]
    rows, width = pieces[0].shape
    runs = len(pieces)
    step = chunk_of(height // 128, 4) * 128

    def kernel(run_ref, inputs_ref, *refs):
        out_ref, all_ref = refs[-2:]

        @pl.when(pl.program_id(0) == 0)
        def _():
            for s in range(runs):
                first = pl.multiple_of(run_ref[s] * rows, rows)
                all_ref[pl.ds(first, rows), :] = refs[s][...]

        out_ref[...] = dot_tn(inputs_ref[...], all_ref[...]) * scale

    return pl.pallas_call(
        kernel,
        grid_spec=pltpu.PrefetchScalarGridSpec(
            num_scalar_prefetch=1,
            grid=(height // step,),
            in_specs=[pl.BlockSpec((tokens, step), lambda i, *_: (0, i))]
            + [whole((rows, width))] * runs
            + [ANY] * len(after),
            out_specs=pl.BlockSpec((step, width), lambda i, *_: (i, 0)),
            scratch_shapes=[pltpu.VMEM((tokens, width), BF16)],
        ),
        out_shape=jax.ShapeDtypeStruct((height, width), F32),
        compiler_params=params(),
        name="up_gradient",
        cost_estimate=cost(gathered, jax.ShapeDtypeStruct((height, width), F32)),
    )(run_rows, gathered, *pieces, *after)


def down_gradient(mixed_all, gathered, run, share, scale, after=()):
    tokens, width = gathered.shape[0], gathered.shape[1] // 2
    if share % 128 == 0:
        step = chunk_of(share // 128, 4) * 128
        first = run * (share // step)
    else:
        mixed_all = lax.dynamic_slice_in_dim(mixed_all, run * share, share, 1)
        step, first = share, run * 0

    def kernel(first_ref, mixed_ref, right_ref, *refs):
        activated = gelu_tanh(mixed_ref[...].astype(F32)).astype(BF16)
        refs[-1][...] = dot_tn(activated, right_ref[...]) * scale

    return pl.pallas_call(
        kernel,
        grid_spec=pltpu.PrefetchScalarGridSpec(
            num_scalar_prefetch=1,
            grid=(share // step,),
            in_specs=[
                pl.BlockSpec((tokens, step), lambda i, first: (0, first[0] + i)),
                column_half(tokens, width, 1),
            ]
            + [ANY] * len(after),
            out_specs=pl.BlockSpec((step, width), lambda i, *_: (i, 0)),
        ),
        out_shape=jax.ShapeDtypeStruct((share, width), F32),
        compiler_params=params(),
        name="down_gradient",
        cost_estimate=cost(gathered, jax.ShapeDtypeStruct((share, width), F32)),
    )(first[None], mixed_all, gathered, *after)


def down_gradient_split(mixed_all, act_rest, gathered, run, share, scale, after=()):
    tokens, width = gathered.shape[0], gathered.shape[1] // 2
    again, size, _ = act_rest.shape
    kept = mixed_all.shape[1] // size
    count = share // size

    def kernel(run_ref, mixed_ref, act_ref, right_ref, *refs):
        out_ref = refs[-1]
        block = run_ref[0] * count + pl.program_id(0)

        @pl.when(block < kept)
        def _():
            activated = gelu_tanh(mixed_ref[...].astype(F32)).astype(BF16)
            out_ref[...] = dot_tn(activated, right_ref[...]) * scale

        @pl.when(block >= kept)
        def _():
            out_ref[...] = dot(act_ref[0], right_ref[...]) * scale

    return pl.pallas_call(
        kernel,
        grid_spec=pltpu.PrefetchScalarGridSpec(
            num_scalar_prefetch=1,
            grid=(count,),
            in_specs=[
                pl.BlockSpec(
                    (tokens, size), lambda i, run: (0, jnp.minimum(run[0] * count + i, kept - 1))
                ),
                pl.BlockSpec(
                    (1, size, tokens),
                    lambda i, run: (jnp.clip(run[0] * count + i - kept, 0, again - 1), 0, 0),
                ),
                column_half(tokens, width, 1),
            ]
            + [ANY] * len(after),
            out_specs=pl.BlockSpec((size, width), lambda i, *_: (i, 0)),
        ),
        out_shape=jax.ShapeDtypeStruct((share, width), F32),
        compiler_params=params(),
        name="down_gradient_split",
        cost_estimate=cost(gathered, jax.ShapeDtypeStruct((share, width), F32)),
    )(run, mixed_all, act_rest, gathered, *after)


def exchanged(value, axis):
    size = lax.axis_size(axis)
    me = lax.axis_index(axis)
    share = value.shape[1] // size
    pieces = []
    for s in range(size):
        piece = lax.dynamic_slice_in_dim(value, ((me + s) % size) * share, share, 1)
        pieces.append(rotated(piece, axis, s) if s else piece)
    return pieces


def body(inputs, out_grad, up_weight, mix_weight, output_factor_matrix, partner, local_perm):
    rows = inputs.shape[0]
    blocks, size = mix_weight.shape[1], mix_weight.shape[2]
    levels = partner.shape[0]
    up, down = up_weight[0], output_factor_matrix[0]
    width = up.shape[1]
    runs = lax.axis_size("dp")
    me, run = lax.axis_index("mp"), lax.axis_index("dp")
    base = me * blocks
    scale = (rows * runs) ** (-0.5)
    run_rows = ((run - jnp.arange(runs, dtype=jnp.int32)) % runs).astype(jnp.int32)
    perm_here = lax.dynamic_slice_in_dim(local_perm, base, blocks, 0) - base
    far_here = lax.dynamic_slice_in_dim(partner, base, blocks, 1)
    far_base = jnp.stack([jnp.bitwise_xor(me, 1 << lv) * blocks for lv in range(levels)])
    far_index = far_here - far_base[:, None]
    index = jnp.concatenate(
        [jnp.arange(blocks, dtype=jnp.int32)[None], perm_here[None], far_index], axis=0
    )
    which = [0, 0] + list(range(1, levels + 1))
    last = levels + 1
    part, share = size // runs, width // runs

    again = blocks // 3 if share % size == 0 else 0
    kept = blocks - again
    theirs = jnp.stack(
        [
            lax.dynamic_slice_in_dim(partner[lv], far_base[lv], blocks, 0) - base
            for lv in range(levels)
        ]
    )

    order = jnp.arange(blocks, dtype=jnp.int32)
    places = jnp.sum(
        jnp.where(theirs[:, None, :] == order[None, :, None], order[None, None, :], 0),
        axis=2,
        dtype=jnp.int32,
    )

    gathered = lax.all_gather(
        jnp.concatenate([inputs, out_grad], axis=1), "dp", axis=0, tiled=True
    )
    hidden = dense(inputs, up, BF16)
    received = [from_partner(hidden, "mp", lv) for lv in range(levels)]
    act_grad = dense(out_grad, down, F32, True, after=received[:-1])
    near = mixed_near(
        [hidden] + received[:-1], which[:-1], index[:-1], list(range(last)), mix_weight,
        after=(act_grad,),
    )
    mixed, activated, delta = mixed_last(
        received[-1], index[-1], last, mix_weight, near, act_grad, kept
    )
    mixed_all = lax.all_gather(mixed, "dp", axis=0, tiled=True)
    far = far_terms(delta, far_index, list(range(2, levels + 2)), mix_weight)
    far_received = [from_partner(far[lv], "mp", lv) for lv in range(levels)]
    hidden_all, hidden_part, *sent = hidden_rows(
        up, gathered, run[None], places, blocks, kept, part, after=far[:1]
    )
    sources = [from_partner(sent[lv], "mp", lv) for lv in range(levels)]
    back = near_terms(delta, perm_here, mix_weight, after=(hidden_part,))
    outputs, act_grad_all = down_pass(
        activated, down, inputs, gathered, kept * size, after=(back,)
    )

    for term in far_received:
        back = back + term.astype(F32)
    hidden_grad = back.astype(BF16)
    hidden_grad_pieces = exchanged(hidden_grad, "dp")
    input_grad = dense_added(hidden_grad, up, out_grad, True, after=(outputs,))
    made, act_rest = None, input_grad
    if again:
        made, act_rest = recomputed(
            hidden_all, sources, again, perm_here, down, gathered, run[None], mix_weight,
            scale, after=(input_grad,),
        )
    up_grad = up_gradient(
        gathered, up.shape[0], hidden_grad_pieces, run_rows, scale, after=(act_rest,)
    )
    if again:
        down_grad = down_gradient_split(
            mixed_all, act_rest, gathered, run[None], share, scale, after=(up_grad,)
        )
    else:
        down_grad = down_gradient(mixed_all, gathered, run, share, scale, after=(up_grad,))
    mix_grad = mix_gradient(
        mixed_all, act_grad_all, hidden_part, sources, perm_here, scale, made
    )
    return (outputs, input_grad, up_grad[None], mix_grad, down_grad[None])


def solution(mesh):
    return jax.shard_map(
        body,
        mesh=mesh,
        in_specs=(
            P(("groups", "dp"), "mp"),
            P(("groups", "dp"), "mp"),
            P("mp", None, None),
            P(None, "mp", None, None),
            P("mp", None, None),
            P(),
            P(),
        ),
        out_specs=(
            P(("groups", "dp"), "mp"),
            P(("groups", "dp"), "mp"),
            P(("groups", "mp"), None, "dp"),
            P("groups", "mp", "dp", None),
            P(("groups", "mp"), "dp", None),
        ),
        check_vma=False,
    )
```

```python
import functools
import math

import jax
import jax.numpy as jnp
from jax import lax
from jax.experimental import pallas as pl
from jax.experimental.pallas import tpu as pltpu
from jax.sharding import PartitionSpec as P

F32 = jnp.float32
BF16 = jnp.bfloat16
VMEM_BYTES = 56 * 1024 * 1024
ANY = pl.BlockSpec(memory_space=pl.ANY)


def from_partner(value, axis, apart):
    mask = 2**apart
    pairs = [(source, source ^ mask) for source in range(lax.axis_size(axis))]
    return lax.ppermute(value, axis, pairs)


def rotated(value, axis, shift):
    size = lax.axis_size(axis)
    return lax.ppermute(value, axis, [(i, (i + shift) % size) for i in range(size)])


def gelu_tanh(values):
    inner = 0.7978845608028654 * (values + 0.044715 * values * values * values)
    return 0.5 * values * (1.0 + jnp.tanh(inner))


def gelu_slope(values):
    inner = 0.7978845608028654 * (values + 0.044715 * values * values * values)
    tangent = jnp.tanh(inner)
    return 0.5 * (1.0 + tangent) + 0.5 * values * (1.0 - tangent * tangent) * 0.7978845608028654 * (
        1.0 + 3.0 * 0.044715 * values * values
    )


def dot(a, b):
    return jnp.dot(a, b, preferred_element_type=F32)


def dot_nt(a, b):
    return lax.dot_general(a, b, (((1,), (1,)), ((), ())), preferred_element_type=F32)


def dot_tn(a, b):
    return lax.dot_general(a, b, (((0,), (0,)), ((), ())), preferred_element_type=F32)


def params():
    return pltpu.CompilerParams(vmem_limit_bytes=VMEM_BYTES)


def cost(*arrays):
    moved = sum(math.prod(a.shape) * a.dtype.itemsize for a in arrays)
    return pl.CostEstimate(flops=0, bytes_accessed=int(2.2 * moved), transcendentals=0)


def level_shape(mix_weight):
    return jax.ShapeDtypeStruct(mix_weight.shape[1:], mix_weight.dtype)


def chunk_of(block_count, most):
    return max(c for c in range(1, most + 1) if block_count % c == 0)


def lanes(index, size):
    return pl.ds(pl.multiple_of(index * size, size), size)


def whole(shape):
    return pl.BlockSpec(shape, lambda i, *_: (0,) * len(shape))


def column_half(tokens, features, half):
    return pl.BlockSpec((tokens, features), lambda i, *_: (0, half))


def weight_specs(levels, chunk, size):
    return [
        pl.BlockSpec((1, chunk, size, size), functools.partial(lambda lv, i, *_: (lv, i, 0, 0), lv))
        for lv in levels
    ]


def mixed_near(sources, which, index, levels, mix_weight, after=()):
    rows, width = sources[0].shape
    blocks, size = mix_weight.shape[1], mix_weight.shape[2]
    chunk = chunk_of(blocks, 4)
    count = len(levels)
    near_shape = jax.ShapeDtypeStruct((rows, width), F32)

    def kernel(index_ref, *refs):
        source_refs, weight_refs, out_ref = refs[: len(sources)], refs[len(sources) :], refs[-1]
        step = pl.program_id(0)
        for c in range(chunk):
            total = None
            for k in range(count):
                picked = source_refs[which[k]][:, lanes(index_ref[k, step * chunk + c], size)]
                term = dot(picked, weight_refs[k][0, c])
                total = term if total is None else total + term
            out_ref[:, c * size : (c + 1) * size] = total

    return pl.pallas_call(
        kernel,
        grid_spec=pltpu.PrefetchScalarGridSpec(
            num_scalar_prefetch=1,
            grid=(blocks // chunk,),
            in_specs=[whole((rows, width)) for _ in sources]
            + weight_specs(levels, chunk, size)
            + [ANY] * len(after),
            out_specs=pl.BlockSpec((rows, chunk * size), lambda i, *_: (0, i)),
        ),
        out_shape=near_shape,
        compiler_params=params(),
        name="mixed_near",
        cost_estimate=cost(*sources, *[level_shape(mix_weight)] * count, near_shape),
    )(index, *sources, *([mix_weight] * count), *after)


def mixed_last(source, index, level, mix_weight, near, act_grad, kept, after=()):
    rows, width = source.shape
    blocks, size = mix_weight.shape[1], mix_weight.shape[2]
    chunk = chunk_of(math.gcd(blocks, kept), 4)

    def kernel(index_ref, source_ref, weight_ref, near_ref, grad_ref, *refs):
        mixed_ref, act_ref, delta_ref = refs[-3:]
        step = pl.program_id(0)
        for c in range(chunk):
            here = slice(c * size, (c + 1) * size)
            picked = source_ref[:, lanes(index_ref[step * chunk + c], size)]
            total = near_ref[:, here] + dot(picked, weight_ref[0, c])

            @pl.when(step < kept // chunk)
            def _(total=total, here=here):
                mixed_ref[:, here] = total.astype(BF16)

            act_ref[:, here] = gelu_tanh(total).astype(BF16)
            delta_ref[:, here] = (grad_ref[:, here] * gelu_slope(total)).astype(BF16)

    columns = pl.BlockSpec((rows, chunk * size), lambda i, *_: (0, i))
    return pl.pallas_call(
        kernel,
        grid_spec=pltpu.PrefetchScalarGridSpec(
            num_scalar_prefetch=1,
            grid=(blocks // chunk,),
            in_specs=[whole((rows, width))] + weight_specs([level], chunk, size)
            + [columns, columns]
            + [ANY] * len(after),
            out_specs=[
                pl.BlockSpec((rows, chunk * size), lambda i, *_: (0, jnp.minimum(i, kept // chunk - 1))),
                columns,
                columns,
            ],
        ),
        out_shape=[jax.ShapeDtypeStruct((rows, kept * size), BF16)]
        + [jax.ShapeDtypeStruct((rows, width), BF16)] * 2,
        compiler_params=params(),
        name="mixed_last",
        cost_estimate=cost(source, level_shape(mix_weight), near, act_grad, source, source),
    )(index, source, mix_weight, near, act_grad, *after)


def far_terms(delta, targets, levels, mix_weight, after=()):
    rows, width = delta.shape
    blocks, size = mix_weight.shape[1], mix_weight.shape[2]
    chunk = chunk_of(blocks, 4)
    count = len(levels)

    def kernel(target_ref, delta_ref, *refs):
        step = pl.program_id(0)
        for c in range(chunk):
            here = delta_ref[:, c * size : (c + 1) * size]
            for k in range(count):
                place = lanes(target_ref[k, step * chunk + c], size)
                refs[count + len(after) + k][:, place] = dot_nt(here, refs[k][0, c]).astype(BF16)

    return pl.pallas_call(
        kernel,
        grid_spec=pltpu.PrefetchScalarGridSpec(
            num_scalar_prefetch=1,
            grid=(blocks // chunk,),
            in_specs=[pl.BlockSpec((rows, chunk * size), lambda i, *_: (0, i))]
            + weight_specs(levels, chunk, size)
            + [ANY] * len(after),
            out_specs=[whole((rows, width))] * count,
        ),
        out_shape=[jax.ShapeDtypeStruct((rows, width), BF16)] * count,
        compiler_params=params(),
        name="far_terms",
        cost_estimate=cost(delta, *[level_shape(mix_weight), delta] * count),
    )(targets, delta, *([mix_weight] * count), *after)


def back_pass(delta, perm, mix_weight, terms, run_next, after=()):
    rows, width = delta.shape
    blocks, size = mix_weight.shape[1], mix_weight.shape[2]
    chunk = chunk_of(blocks, 4)
    runs = run_next.shape[0]
    share = width // runs
    split = share % 128 == 0

    def kernel(perm_ref, run_ref, delta_ref, own_ref, perm_weight_ref, *refs):
        out_ref, *piece_refs, total_ref = refs[len(terms) + len(after) :]
        step = pl.program_id(0)

        @pl.when(step == 0)
        def _():
            total = refs[0][...].astype(F32)
            for term_ref in refs[1 : len(terms)]:
                total = total + term_ref[...].astype(F32)
            total_ref[...] = total

        for c in range(chunk):
            here = delta_ref[:, c * size : (c + 1) * size]
            total_ref[:, lanes(step * chunk + c, size)] += dot_nt(here, own_ref[0, c])
            total_ref[:, lanes(perm_ref[step * chunk + c], size)] += dot_nt(here, perm_weight_ref[0, c])

        @pl.when(step == blocks // chunk - 1)
        def _():
            out_ref[...] = total_ref[...].astype(BF16)
            for s, piece_ref in enumerate(piece_refs):
                piece_ref[...] = total_ref[:, lanes(run_ref[s], share)].astype(BF16)

    results = pl.pallas_call(
        kernel,
        grid_spec=pltpu.PrefetchScalarGridSpec(
            num_scalar_prefetch=2,
            grid=(blocks // chunk,),
            in_specs=[pl.BlockSpec((rows, chunk * size), lambda i, *_: (0, i))]
            + weight_specs([0, 1], chunk, size)
            + [whole((rows, width))] * len(terms)
            + [ANY] * len(after),
            out_specs=[whole((rows, width))] + [whole((rows, share))] * (runs if split else 0),
            scratch_shapes=[pltpu.VMEM((rows, width), F32)],
        ),
        out_shape=[jax.ShapeDtypeStruct((rows, width), BF16)]
        + [jax.ShapeDtypeStruct((rows, share), BF16)] * (runs if split else 0),
        compiler_params=params(),
        name="back_pass",
        cost_estimate=cost(delta, *terms, *[level_shape(mix_weight)] * 2),
    )(perm, run_next, delta, mix_weight, mix_weight, *terms, *after)
    if split:
        return results[0], results[1:]
    return results[0], [
        lax.dynamic_slice_in_dim(results[0], run_next[s] * share, share, 1) for s in range(runs)
    ]


def dense(left, right, out_type, right_transposed=False, after=()):
    rows, depth = left.shape
    width = right.shape[0] if right_transposed else right.shape[1]
    step = chunk_of(width // 128, 12) * 128
    out_shape = jax.ShapeDtypeStruct((rows, width), out_type)
    if right_transposed:
        right_spec = pl.BlockSpec((step, depth), lambda i: (i, 0))
    else:
        right_spec = pl.BlockSpec((depth, step), lambda i: (0, i))

    def kernel(left_ref, right_ref, *refs):
        product = (dot_nt if right_transposed else dot)(left_ref[...], right_ref[...])
        refs[-1][...] = product.astype(out_type)

    return pl.pallas_call(
        kernel,
        grid=(width // step,),
        in_specs=[whole((rows, depth)), right_spec] + [ANY] * len(after),
        out_specs=pl.BlockSpec((rows, step), lambda i: (0, i)),
        out_shape=out_shape,
        compiler_params=params(),
        name="dense_nt" if right_transposed else "dense",
        cost_estimate=cost(left, right, out_shape),
    )(left, right, *after)


def dense_added(left, right, base, right_transposed=False, after=()):
    rows, depth = left.shape
    width = base.shape[1]
    step = chunk_of(depth // 128, 12) * 128
    if right_transposed:
        right_spec = pl.BlockSpec((width, step), lambda i: (0, i))
    else:
        right_spec = pl.BlockSpec((step, width), lambda i: (i, 0))

    def kernel(left_ref, right_ref, base_ref, *refs):
        out_ref, total_ref = refs[-2], refs[-1]
        here = pl.program_id(0)

        @pl.when(here == 0)
        def _():
            total_ref[...] = base_ref[...].astype(F32)

        total_ref[...] += (dot_nt if right_transposed else dot)(left_ref[...], right_ref[...])

        @pl.when(here == depth // step - 1)
        def _():
            out_ref[...] = total_ref[...].astype(out_ref.dtype)

    return pl.pallas_call(
        kernel,
        grid=(depth // step,),
        in_specs=[pl.BlockSpec((rows, step), lambda i: (0, i)), right_spec, whole(base.shape)]
        + [ANY] * len(after),
        out_specs=whole(base.shape),
        out_shape=jax.ShapeDtypeStruct(base.shape, base.dtype),
        scratch_shapes=[pltpu.VMEM(base.shape, F32)],
        compiler_params=params(),
        name="added_nt" if right_transposed else "added",
        cost_estimate=cost(left, right, base),
    )(left, right, base, *after)


def hidden_rows(up, gathered, run_rows, places, blocks, kept, part, rows, after=()):
    depth, width = up.shape
    tokens = gathered.shape[0]
    size = width // blocks
    chunk = chunk_of(blocks, 4)
    levels = places.shape[0]
    again = blocks - kept
    others = tokens - rows
    sent = [jax.ShapeDtypeStruct((kept * part, tokens), BF16)] * levels
    if again:
        sent += [jax.ShapeDtypeStruct((again * size, others), BF16)] * levels

    def kernel(run_ref, place_ref, up_ref, inputs_ref, *refs):
        whole_ref, out_ref, *sent_refs, full_ref = refs[len(after) :]
        full_ref[...] = dot(inputs_ref[...], up_ref[...]).astype(BF16).T
        for c in range(chunk):
            first = pl.multiple_of(run_ref[0] * part, part) + c * size
            for s in range(1, tokens // rows):
                there = pl.multiple_of(run_ref[s] * rows, rows)
                piece = full_ref[c * size : (c + 1) * size, pl.ds(there, rows)]
                whole_ref[c, :, (s - 1) * rows : s * rows] = piece
            out_ref[c] = full_ref[pl.ds(first, part), :]
            for lv in range(levels):
                place = place_ref[lv, pl.program_id(0) * chunk + c]

                if again:

                    @pl.when(place >= kept)
                    def _(place=place, lv=lv, c=c):
                        there = pl.multiple_of((place - kept) * size, size)
                        sent_refs[levels + lv][pl.ds(there, size), :] = whole_ref[c]

                @pl.when(place < kept)
                def _(place=place, lv=lv, c=c):
                    there = pl.multiple_of(place * part, part)
                    sent_refs[lv][pl.ds(there, part), :] = out_ref[c]

    return pl.pallas_call(
        kernel,
        grid_spec=pltpu.PrefetchScalarGridSpec(
            num_scalar_prefetch=2,
            grid=(blocks // chunk,),
            in_specs=[
                pl.BlockSpec((depth, chunk * size), lambda i, *_: (0, i)),
                column_half(tokens, depth, 0),
            ]
            + [ANY] * len(after),
            out_specs=[
                pl.BlockSpec((chunk, size, others), lambda i, *_: (i, 0, 0)),
                pl.BlockSpec((chunk, part, tokens), lambda i, *_: (i, 0, 0)),
            ]
            + [whole(shape.shape) for shape in sent],
            scratch_shapes=[pltpu.VMEM((chunk * size, tokens), BF16)],
        ),
        out_shape=[
            jax.ShapeDtypeStruct((blocks, size, others), BF16),
            jax.ShapeDtypeStruct((blocks, part, tokens), BF16),
        ]
        + sent,
        compiler_params=params(),
        name="hidden_rows",
        cost_estimate=cost(up, jax.ShapeDtypeStruct((blocks, size, tokens), BF16)),
    )(run_rows, places, up, gathered, *after)


def down_first(activated, down, base, gathered, kept, after=()):
    rows, width = activated.shape
    features = down.shape[1]
    tokens = gathered.shape[0]
    step = chunk_of(math.gcd(width, kept) // 128, 8) * 128
    out_type = BF16 if kept == width else F32

    def kernel(act_ref, down_ref, base_ref, all_ref, *refs):
        out_ref, grad_ref, total_ref = refs[-3:]
        here = pl.program_id(0)

        @pl.when(here == 0)
        def _():
            total_ref[...] = base_ref[...].astype(F32)

        total_ref[...] += dot(act_ref[...], down_ref[...])
        grad_ref[...] = dot_nt(all_ref[...], down_ref[...])

        @pl.when(here == kept // step - 1)
        def _():
            out_ref[...] = total_ref[...].astype(out_type)

    out_shape = [
        jax.ShapeDtypeStruct((rows, features), out_type),
        jax.ShapeDtypeStruct((tokens, kept), F32),
    ]
    return pl.pallas_call(
        kernel,
        grid=(kept // step,),
        in_specs=[
            pl.BlockSpec((rows, step), lambda i: (0, i)),
            pl.BlockSpec((step, features), lambda i: (i, 0)),
            whole((rows, features)),
            column_half(tokens, features, 1),
        ]
        + [ANY] * len(after),
        out_specs=[
            whole((rows, features)),
            pl.BlockSpec((tokens, step), lambda i: (0, i)),
        ],
        out_shape=out_shape,
        scratch_shapes=[pltpu.VMEM((rows, features), F32)],
        compiler_params=params(),
        name="down_first",
        cost_estimate=cost(activated, down, out_shape[1]),
    )(activated, down, base, gathered, *after)


def down_rest(activated, down, partial, gathered, run_rows, kept, after=()):
    rows, width = activated.shape
    features = down.shape[1]
    tokens = gathered.shape[0]
    others = tokens - rows
    step = chunk_of(math.gcd(width, kept) // 128, 8) * 128
    first = kept // step

    def kernel(run_ref, act_ref, down_ref, partial_ref, all_ref, *refs):
        out_ref, grad_ref, rest_ref, total_ref = refs[-4:]
        here = pl.program_id(0)

        @pl.when(here == 0)
        def _():
            total_ref[...] = partial_ref[...]
            for s in range(1, tokens // rows):
                there = pl.multiple_of(run_ref[s] * rows, rows)
                rest_ref[(s - 1) * rows : s * rows, :] = all_ref[pl.ds(there, rows), :]

        total_ref[...] += dot(act_ref[...], down_ref[...])
        grad_ref[...] = dot_nt(down_ref[...], rest_ref[...])

        @pl.when(here == width // step - first - 1)
        def _():
            out_ref[...] = total_ref[...].astype(BF16)

    out_shape = [
        jax.ShapeDtypeStruct((rows, features), BF16),
        jax.ShapeDtypeStruct((width - kept, others), F32),
        jax.ShapeDtypeStruct((others, features), BF16),
    ]
    return pl.pallas_call(
        kernel,
        grid_spec=pltpu.PrefetchScalarGridSpec(
            num_scalar_prefetch=1,
            grid=(width // step - first,),
            in_specs=[
                pl.BlockSpec((rows, step), lambda i, *_: (0, first + i)),
                pl.BlockSpec((step, features), lambda i, *_: (first + i, 0)),
                whole((rows, features)),
                column_half(tokens, features, 1),
            ]
            + [ANY] * len(after),
            out_specs=[
                whole((rows, features)),
                pl.BlockSpec((step, others), lambda i, *_: (i, 0)),
                whole((others, features)),
            ],
            scratch_shapes=[pltpu.VMEM((rows, features), F32)],
        ),
        out_shape=out_shape,
        compiler_params=params(),
        name="down_rest",
        cost_estimate=cost(out_shape[1], out_shape[1], partial, partial),
    )(run_rows, activated, down, partial, gathered, *after)


def mix_gradient(mixed_all, act_grad_all, hidden_part, received, perm, scale, made=None):
    tokens, width = mixed_all.shape
    blocks, part, _ = hidden_part.shape
    size = part * lax.axis_size("dp")
    kept = width // size
    chunk = chunk_of(kept, 4)
    count = 2 + len(received)
    given = whole((kept * part, tokens))

    def kernel(perm_ref, mixed_ref, grad_ref, part_ref, *refs):
        given_refs, out_ref = refs[: len(received)], refs[-1]
        step = pl.program_id(0)
        for c in range(chunk):
            here = slice(c * size, (c + 1) * size)
            block = step * chunk + c
            slope = gelu_slope(mixed_ref[:, here].astype(F32))
            delta = (grad_ref[:, here] * slope).astype(BF16)
            rows = pl.ds(pl.multiple_of(block * part, part), part)
            picked = jnp.concatenate(
                [part_ref[block], part_ref[perm_ref[block]]] + [ref[rows, :] for ref in given_refs],
                axis=0,
            )
            result = dot(picked, delta) * scale
            for k in range(count):
                out_ref[k, c] = result[k * part : (k + 1) * part]

    columns = pl.BlockSpec((tokens, chunk * size), lambda i, *_: (0, i))
    return pl.pallas_call(
        kernel,
        grid_spec=pltpu.PrefetchScalarGridSpec(
            num_scalar_prefetch=1,
            grid=(kept // chunk,),
            in_specs=[columns, columns, whole(hidden_part.shape)]
            + [given] * len(received)
            + ([] if made is None else [ANY]),
            out_specs=pl.BlockSpec((count, chunk, part, size), lambda i, *_: (0, i, 0, 0)),
        ),
        out_shape=jax.ShapeDtypeStruct((count, blocks, part, size), F32),
        input_output_aliases={} if made is None else {4 + len(received): 0},
        compiler_params=params(),
        name="mix_gradient",
        cost_estimate=cost(mixed_all, act_grad_all),
    )(perm, mixed_all, act_grad_all, hidden_part, *received, *([] if made is None else [made]))


def recomputed(
    own_sources, own_delta, others, received, index, act_grad_rest, run, mix_weight, scale, after=()
):
    blocks, size, tokens = others.shape
    rows = own_delta.shape[0]
    count = mix_weight.shape[0]
    again = act_grad_rest.shape[0] // size
    kept = blocks - again
    part = size // lax.axis_size("dp")
    chunk = chunk_of(math.gcd(again, kept), 2)

    def kernel(index_ref, run_ref, *refs):
        straight_ref, *refs = refs
        permuted_refs, refs = refs[:chunk], refs[chunk:]
        received_refs, refs = refs[: len(received)], refs[len(received) :]
        own_refs, refs = refs[: count * chunk], refs[count * chunk :]
        weight_refs, refs = refs[:count], refs[count:]
        grad_ref, delta_ref = refs[:2]
        out_ref, act_ref, full_ref = refs[-3:]
        first = pl.multiple_of(run_ref[0] * part, part)
        for c in range(chunk):
            here = pl.ds(c * size, size)
            sources = [straight_ref.at[c], permuted_refs[c].at[0]]
            sources += [ref.at[here] for ref in received_refs]
            mixed = None
            for k in range(count):
                term = dot_tn(weight_refs[k][0, c], sources[k][...])
                mixed = term if mixed is None else mixed + term
                full_ref[c * count + k] = dot_tn(own_refs[k * chunk + c][...], delta_ref[:, here])
            act_ref[c] = gelu_tanh(mixed).astype(BF16)
            delta = (grad_ref[here, :] * gelu_slope(mixed)).astype(BF16)
            picked = jnp.concatenate([ref[pl.ds(first, part), :] for ref in sources], axis=0)
            result = dot_nt(picked, delta)
            for k in range(count):
                own = full_ref[c * count + k, pl.ds(first, part), :]
                out_ref[k, c] = (result[k * part : (k + 1) * part] + own) * scale

    source_specs = [
        pl.BlockSpec((chunk, size, tokens), lambda i, *_: (kept // chunk + i, 0, 0))
    ]
    for c in range(chunk):
        source_specs.append(
            pl.BlockSpec(
                (1, size, tokens),
                functools.partial(lambda c, i, index, run: (index[1, kept + i * chunk + c], 0, 0), c),
            )
        )
    source_specs += [pl.BlockSpec((chunk * size, tokens), lambda i, *_: (i, 0))] * len(received)
    own_specs = [
        pl.BlockSpec(
            (rows, size),
            functools.partial(
                lambda k, c, i, index, run: (0, index[k, kept + i * chunk + c]), k, c
            ),
        )
        for k in range(count)
        for c in range(chunk)
    ]
    level_specs = [
        pl.BlockSpec(
            (1, chunk, size, size),
            functools.partial(lambda k, i, *_: (k, kept // chunk + i, 0, 0), k),
        )
        for k in range(count)
    ]
    return pl.pallas_call(
        kernel,
        grid_spec=pltpu.PrefetchScalarGridSpec(
            num_scalar_prefetch=2,
            grid=(again // chunk,),
            in_specs=source_specs
            + own_specs
            + level_specs
            + [
                pl.BlockSpec((chunk * size, tokens), lambda i, *_: (i, 0)),
                pl.BlockSpec((rows, chunk * size), lambda i, *_: (0, kept // chunk + i)),
            ]
            + [ANY] * len(after),
            out_specs=[
                pl.BlockSpec((count, chunk, part, size), lambda i, *_: (0, kept // chunk + i, 0, 0)),
                pl.BlockSpec((chunk, size, tokens), lambda i, *_: (i, 0, 0)),
            ],
            scratch_shapes=[pltpu.VMEM((chunk * count, size, size), F32)],
        ),
        out_shape=[
            jax.ShapeDtypeStruct((count, blocks, part, size), F32),
            jax.ShapeDtypeStruct((again, size, tokens), BF16),
        ],
        compiler_params=params(),
        name="recomputed",
        cost_estimate=cost(*received, *received, act_grad_rest),
    )(
        index, run, others, *([others] * chunk), *received,
        *[source for source in own_sources for _ in range(chunk)], *([mix_weight] * count),
        act_grad_rest, own_delta, *after,
    )


def up_gradient(gathered, height, pieces, run_rows, scale, after=()):
    tokens = gathered.shape[0]
    rows, width = pieces[0].shape
    runs = len(pieces)
    step = chunk_of(height // 128, 4) * 128

    def kernel(run_ref, inputs_ref, *refs):
        out_ref, all_ref = refs[-2:]

        @pl.when(pl.program_id(0) == 0)
        def _():
            for s in range(runs):
                first = pl.multiple_of(run_ref[s] * rows, rows)
                all_ref[pl.ds(first, rows), :] = refs[s][...]

        out_ref[...] = dot_tn(inputs_ref[...], all_ref[...]) * scale

    return pl.pallas_call(
        kernel,
        grid_spec=pltpu.PrefetchScalarGridSpec(
            num_scalar_prefetch=1,
            grid=(height // step,),
            in_specs=[pl.BlockSpec((tokens, step), lambda i, *_: (0, i))]
            + [whole((rows, width))] * runs
            + [ANY] * len(after),
            out_specs=pl.BlockSpec((step, width), lambda i, *_: (i, 0)),
            scratch_shapes=[pltpu.VMEM((tokens, width), BF16)],
        ),
        out_shape=jax.ShapeDtypeStruct((height, width), F32),
        compiler_params=params(),
        name="up_gradient",
        cost_estimate=cost(gathered, jax.ShapeDtypeStruct((height, width), F32)),
    )(run_rows, gathered, *pieces, *after)


def down_gradient(mixed_all, gathered, run, share, scale, after=()):
    tokens, width = gathered.shape[0], gathered.shape[1] // 2
    if share % 128 == 0:
        step = chunk_of(share // 128, 4) * 128
        first = run * (share // step)
    else:
        mixed_all = lax.dynamic_slice_in_dim(mixed_all, run * share, share, 1)
        step, first = share, run * 0

    def kernel(first_ref, mixed_ref, right_ref, *refs):
        activated = gelu_tanh(mixed_ref[...].astype(F32)).astype(BF16)
        refs[-1][...] = dot_tn(activated, right_ref[...]) * scale

    return pl.pallas_call(
        kernel,
        grid_spec=pltpu.PrefetchScalarGridSpec(
            num_scalar_prefetch=1,
            grid=(share // step,),
            in_specs=[
                pl.BlockSpec((tokens, step), lambda i, first: (0, first[0] + i)),
                column_half(tokens, width, 1),
            ]
            + [ANY] * len(after),
            out_specs=pl.BlockSpec((step, width), lambda i, *_: (i, 0)),
        ),
        out_shape=jax.ShapeDtypeStruct((share, width), F32),
        compiler_params=params(),
        name="down_gradient",
        cost_estimate=cost(gathered, jax.ShapeDtypeStruct((share, width), F32)),
    )(first[None], mixed_all, gathered, *after)


def down_gradient_split(
    mixed_all, act_rest, activated, gathered, own, rest, run, share, scale, after=()
):
    tokens, width = gathered.shape[0], gathered.shape[1] // 2
    again, size, others = act_rest.shape
    rows, kept = activated.shape[0], mixed_all.shape[1] // size
    count = share // size

    def kernel(run_ref, mixed_ref, act_ref, own_act_ref, right_ref, own_ref, rest_ref, *refs):
        out_ref = refs[-1]
        block = run_ref[0] * count + pl.program_id(0)

        @pl.when(block < kept)
        def _():
            act = gelu_tanh(mixed_ref[...].astype(F32)).astype(BF16)
            out_ref[...] = dot_tn(act, right_ref[...]) * scale

        @pl.when(block >= kept)
        def _():
            total = dot(act_ref[0], rest_ref[...]) + dot_tn(own_act_ref[...], own_ref[...])
            out_ref[...] = total * scale

    return pl.pallas_call(
        kernel,
        grid_spec=pltpu.PrefetchScalarGridSpec(
            num_scalar_prefetch=1,
            grid=(count,),
            in_specs=[
                pl.BlockSpec(
                    (tokens, size), lambda i, run: (0, jnp.minimum(run[0] * count + i, kept - 1))
                ),
                pl.BlockSpec(
                    (1, size, others),
                    lambda i, run: (jnp.clip(run[0] * count + i - kept, 0, again - 1), 0, 0),
                ),
                pl.BlockSpec((rows, size), lambda i, run: (0, run[0] * count + i)),
                column_half(tokens, width, 1),
                whole((rows, width)),
                whole((others, width)),
            ]
            + [ANY] * len(after),
            out_specs=pl.BlockSpec((size, width), lambda i, *_: (i, 0)),
        ),
        out_shape=jax.ShapeDtypeStruct((share, width), F32),
        compiler_params=params(),
        name="down_gradient_split",
        cost_estimate=cost(gathered, jax.ShapeDtypeStruct((share, width), F32)),
    )(run, mixed_all, act_rest, activated, gathered, own, rest, *after)


def body(inputs, out_grad, up_weight, mix_weight, output_factor_matrix, partner, local_perm):
    rows = inputs.shape[0]
    blocks, size = mix_weight.shape[1], mix_weight.shape[2]
    levels = partner.shape[0]
    up, down = up_weight[0], output_factor_matrix[0]
    width = up.shape[1]
    runs = lax.axis_size("dp")
    me, run = lax.axis_index("mp"), lax.axis_index("dp")
    base = me * blocks
    scale = (rows * runs) ** (-0.5)
    run_rows = ((run - jnp.arange(runs, dtype=jnp.int32)) % runs).astype(jnp.int32)
    perm_here = lax.dynamic_slice_in_dim(local_perm, base, blocks, 0) - base
    far_here = lax.dynamic_slice_in_dim(partner, base, blocks, 1)
    far_base = jnp.stack([jnp.bitwise_xor(me, 1 << lv) * blocks for lv in range(levels)])
    far_index = far_here - far_base[:, None]
    index = jnp.concatenate(
        [jnp.arange(blocks, dtype=jnp.int32)[None], perm_here[None], far_index], axis=0
    )
    which = [0, 0] + list(range(1, levels + 1))
    last = levels + 1
    part, share = size // runs, width // runs

    again = blocks // 3 if share % size == 0 else 0
    kept = blocks - again
    theirs = jnp.stack(
        [
            lax.dynamic_slice_in_dim(partner[lv], far_base[lv], blocks, 0) - base
            for lv in range(levels)
        ]
    )

    order = jnp.arange(blocks, dtype=jnp.int32)
    places = jnp.sum(
        jnp.where(theirs[:, None, :] == order[None, :, None], order[None, None, :], 0),
        axis=2,
        dtype=jnp.int32,
    )

    gathered = lax.all_gather(
        jnp.concatenate([inputs, out_grad], axis=1), "dp", axis=0, tiled=True
    )
    hidden = dense(inputs, up, BF16)
    received = [from_partner(hidden, "mp", lv) for lv in range(levels)]
    act_grad = dense(out_grad, down, F32, True, after=received[:-1])
    near = mixed_near(
        [hidden] + received[:-1], which[:-1], index[:-1], list(range(last)), mix_weight,
        after=(act_grad,),
    )
    mixed, activated, delta = mixed_last(
        received[-1], index[-1], last, mix_weight, near, act_grad, kept
    )
    mixed_all = lax.all_gather(mixed, "dp", axis=0, tiled=True)
    far = far_terms(delta, far_index, list(range(2, levels + 2)), mix_weight)
    far_received = [from_partner(far[lv], "mp", lv) for lv in range(levels)]
    outputs, act_grad_all = down_first(
        activated, down, inputs, gathered, kept * size, after=far[:1]
    )
    others, hidden_part, *sent = hidden_rows(
        up, gathered, run_rows, places, blocks, kept, part, rows,
        after=[outputs] + far_received[:1],
    )
    sources = [from_partner(piece, "mp", k % levels) for k, piece in enumerate(sent)]
    part_sources, whole_sources = sources[:levels], sources[levels:]
    run_next = ((run + jnp.arange(runs, dtype=jnp.int32)) % runs).astype(jnp.int32)
    hidden_grad, to_send = back_pass(
        delta, perm_here, mix_weight, far_received, run_next, after=[hidden_part] + sources[::levels]
    )
    hidden_grad_pieces = [to_send[0]] + [rotated(to_send[s], "dp", s) for s in range(1, runs)]
    rest = None
    if again:
        outputs, *rest = down_rest(
            activated, down, outputs, gathered, run_rows, kept * size, after=(hidden_grad,)
        )
    input_grad = dense_added(hidden_grad, up, out_grad, True, after=(outputs,))
    made, act_rest = None, input_grad
    if again:
        made, act_rest = recomputed(
            [hidden, hidden] + received, delta, others, whole_sources, index, rest[0], run[None],
            mix_weight, scale, after=(input_grad,),
        )
    up_grad = up_gradient(
        gathered, up.shape[0], hidden_grad_pieces, run_rows, scale, after=(act_rest,)
    )
    if again:
        down_grad = down_gradient_split(
            mixed_all, act_rest, activated, gathered, out_grad, rest[1], run[None], share,
            scale, after=(up_grad,),
        )
    else:
        down_grad = down_gradient(mixed_all, gathered, run, share, scale, after=(up_grad,))
    mix_grad = mix_gradient(
        mixed_all, act_grad_all, hidden_part, part_sources, perm_here, scale, made
    )
    return (outputs, input_grad, up_grad[None], mix_grad, down_grad[None])


def solution(mesh):
    return jax.shard_map(
        body,
        mesh=mesh,
        in_specs=(
            P(("groups", "dp"), "mp"),
            P(("groups", "dp"), "mp"),
            P("mp", None, None),
            P(None, "mp", None, None),
            P("mp", None, None),
            P(),
            P(),
        ),
        out_specs=(
            P(("groups", "dp"), "mp"),
            P(("groups", "dp"), "mp"),
            P(("groups", "mp"), None, "dp"),
            P("groups", "mp", "dp", None),
            P(("groups", "mp"), "dp", None),
        ),
        check_vma=False,
    )
```

```python
import functools
import math

import jax
import jax.numpy as jnp
from jax import lax
from jax.experimental import pallas as pl
from jax.experimental.pallas import tpu as pltpu
from jax.sharding import PartitionSpec as P

F32 = jnp.float32
BF16 = jnp.bfloat16
VMEM_BYTES = 56 * 1024 * 1024
ANY = pl.BlockSpec(memory_space=pl.ANY)


def from_partner(value, axis, apart):
    mask = 2**apart
    pairs = [(source, source ^ mask) for source in range(lax.axis_size(axis))]
    return lax.ppermute(value, axis, pairs)


def rotated(value, axis, shift):
    size = lax.axis_size(axis)
    return lax.ppermute(value, axis, [(i, (i + shift) % size) for i in range(size)])


def gelu_tanh(values):
    inner = 0.7978845608028654 * (values + 0.044715 * values * values * values)
    return 0.5 * values * (1.0 + jnp.tanh(inner))


def gelu_slope(values):
    inner = 0.7978845608028654 * (values + 0.044715 * values * values * values)
    tangent = jnp.tanh(inner)
    return 0.5 * (1.0 + tangent) + 0.5 * values * (1.0 - tangent * tangent) * 0.7978845608028654 * (
        1.0 + 3.0 * 0.044715 * values * values
    )


def dot(a, b):
    return jnp.dot(a, b, preferred_element_type=F32)


def dot_nt(a, b):
    return lax.dot_general(a, b, (((1,), (1,)), ((), ())), preferred_element_type=F32)


def dot_tn(a, b):
    return lax.dot_general(a, b, (((0,), (0,)), ((), ())), preferred_element_type=F32)


def params():
    return pltpu.CompilerParams(vmem_limit_bytes=VMEM_BYTES)


def cost(*arrays):
    moved = sum(math.prod(a.shape) * a.dtype.itemsize for a in arrays)
    return pl.CostEstimate(flops=0, bytes_accessed=int(2.2 * moved), transcendentals=0)


def level_shape(mix_weight):
    return jax.ShapeDtypeStruct(mix_weight.shape[1:], mix_weight.dtype)


def chunk_of(block_count, most):
    return max(c for c in range(1, most + 1) if block_count % c == 0)


def lanes(index, size):
    return pl.ds(pl.multiple_of(index * size, size), size)


def whole(shape):
    return pl.BlockSpec(shape, lambda i, *_: (0,) * len(shape))


def column_half(tokens, features, half):
    return pl.BlockSpec((tokens, features), lambda i, *_: (0, half))


def weight_specs(levels, chunk, size):
    return [
        pl.BlockSpec((1, chunk, size, size), functools.partial(lambda lv, i, *_: (lv, i, 0, 0), lv))
        for lv in levels
    ]


def mixed_near(sources, which, index, levels, mix_weight, after=()):
    rows, width = sources[0].shape
    blocks, size = mix_weight.shape[1], mix_weight.shape[2]
    chunk = chunk_of(blocks, 4)
    count = len(levels)
    near_shape = jax.ShapeDtypeStruct((rows, width), F32)

    def kernel(index_ref, *refs):
        source_refs, weight_refs, out_ref = refs[: len(sources)], refs[len(sources) :], refs[-1]
        step = pl.program_id(0)
        for c in range(chunk):
            total = None
            for k in range(count):
                picked = source_refs[which[k]][:, lanes(index_ref[k, step * chunk + c], size)]
                term = dot(picked, weight_refs[k][0, c])
                total = term if total is None else total + term
            out_ref[:, c * size : (c + 1) * size] = total

    return pl.pallas_call(
        kernel,
        grid_spec=pltpu.PrefetchScalarGridSpec(
            num_scalar_prefetch=1,
            grid=(blocks // chunk,),
            in_specs=[whole((rows, width)) for _ in sources]
            + weight_specs(levels, chunk, size)
            + [ANY] * len(after),
            out_specs=pl.BlockSpec((rows, chunk * size), lambda i, *_: (0, i)),
        ),
        out_shape=near_shape,
        compiler_params=params(),
        name="mixed_near",
        cost_estimate=cost(*sources, *[level_shape(mix_weight)] * count, near_shape),
    )(index, *sources, *([mix_weight] * count), *after)


def mixed_last(source, index, level, mix_weight, near, act_grad, kept, after=()):
    rows, width = source.shape
    blocks, size = mix_weight.shape[1], mix_weight.shape[2]
    chunk = chunk_of(math.gcd(blocks, kept), 4)

    def kernel(index_ref, source_ref, weight_ref, near_ref, grad_ref, *refs):
        mixed_ref, act_ref, delta_ref = refs[-3:]
        step = pl.program_id(0)
        for c in range(chunk):
            here = slice(c * size, (c + 1) * size)
            picked = source_ref[:, lanes(index_ref[step * chunk + c], size)]
            total = near_ref[:, here] + dot(picked, weight_ref[0, c])

            @pl.when(step < kept // chunk)
            def _(total=total, here=here):
                mixed_ref[:, here] = total.astype(BF16)

            act_ref[:, here] = gelu_tanh(total).astype(BF16)
            delta_ref[:, here] = (grad_ref[:, here] * gelu_slope(total)).astype(BF16)

    columns = pl.BlockSpec((rows, chunk * size), lambda i, *_: (0, i))
    return pl.pallas_call(
        kernel,
        grid_spec=pltpu.PrefetchScalarGridSpec(
            num_scalar_prefetch=1,
            grid=(blocks // chunk,),
            in_specs=[whole((rows, width))] + weight_specs([level], chunk, size)
            + [columns, columns]
            + [ANY] * len(after),
            out_specs=[
                pl.BlockSpec((rows, chunk * size), lambda i, *_: (0, jnp.minimum(i, kept // chunk - 1))),
                columns,
                columns,
            ],
        ),
        out_shape=[jax.ShapeDtypeStruct((rows, kept * size), BF16)]
        + [jax.ShapeDtypeStruct((rows, width), BF16)] * 2,
        compiler_params=params(),
        name="mixed_last",
        cost_estimate=cost(source, level_shape(mix_weight), near, act_grad, source, source),
    )(index, source, mix_weight, near, act_grad, *after)


def far_terms(delta, targets, levels, mix_weight, after=()):
    rows, width = delta.shape
    blocks, size = mix_weight.shape[1], mix_weight.shape[2]
    chunk = chunk_of(blocks, 4)
    count = len(levels)

    def kernel(target_ref, delta_ref, *refs):
        step = pl.program_id(0)
        for c in range(chunk):
            here = delta_ref[:, c * size : (c + 1) * size]
            for k in range(count):
                place = lanes(target_ref[k, step * chunk + c], size)
                refs[count + len(after) + k][:, place] = dot_nt(here, refs[k][0, c]).astype(BF16)

    return pl.pallas_call(
        kernel,
        grid_spec=pltpu.PrefetchScalarGridSpec(
            num_scalar_prefetch=1,
            grid=(blocks // chunk,),
            in_specs=[pl.BlockSpec((rows, chunk * size), lambda i, *_: (0, i))]
            + weight_specs(levels, chunk, size)
            + [ANY] * len(after),
            out_specs=[whole((rows, width))] * count,
        ),
        out_shape=[jax.ShapeDtypeStruct((rows, width), BF16)] * count,
        compiler_params=params(),
        name="far_terms",
        cost_estimate=cost(delta, *[level_shape(mix_weight), delta] * count),
    )(targets, delta, *([mix_weight] * count), *after)


def back_pass(delta, perm, mix_weight, terms, run_next, after=()):
    rows, width = delta.shape
    blocks, size = mix_weight.shape[1], mix_weight.shape[2]
    chunk = chunk_of(blocks, 4)
    runs = run_next.shape[0]
    share = width // runs
    split = share % 128 == 0

    def kernel(perm_ref, run_ref, delta_ref, own_ref, perm_weight_ref, *refs):
        out_ref, *piece_refs, total_ref = refs[len(terms) + len(after) :]
        step = pl.program_id(0)

        @pl.when(step == 0)
        def _():
            total = refs[0][...].astype(F32)
            for term_ref in refs[1 : len(terms)]:
                total = total + term_ref[...].astype(F32)
            total_ref[...] = total

        for c in range(chunk):
            here = delta_ref[:, c * size : (c + 1) * size]
            total_ref[:, lanes(step * chunk + c, size)] += dot_nt(here, own_ref[0, c])
            total_ref[:, lanes(perm_ref[step * chunk + c], size)] += dot_nt(here, perm_weight_ref[0, c])

        @pl.when(step == blocks // chunk - 1)
        def _():
            out_ref[...] = total_ref[...].astype(BF16)
            for s, piece_ref in enumerate(piece_refs):
                piece_ref[...] = total_ref[:, lanes(run_ref[s], share)].astype(BF16)

    results = pl.pallas_call(
        kernel,
        grid_spec=pltpu.PrefetchScalarGridSpec(
            num_scalar_prefetch=2,
            grid=(blocks // chunk,),
            in_specs=[pl.BlockSpec((rows, chunk * size), lambda i, *_: (0, i))]
            + weight_specs([0, 1], chunk, size)
            + [whole((rows, width))] * len(terms)
            + [ANY] * len(after),
            out_specs=[whole((rows, width))] + [whole((rows, share))] * (runs if split else 0),
            scratch_shapes=[pltpu.VMEM((rows, width), F32)],
        ),
        out_shape=[jax.ShapeDtypeStruct((rows, width), BF16)]
        + [jax.ShapeDtypeStruct((rows, share), BF16)] * (runs if split else 0),
        compiler_params=params(),
        name="back_pass",
        cost_estimate=cost(delta, *terms, *[level_shape(mix_weight)] * 2),
    )(perm, run_next, delta, mix_weight, mix_weight, *terms, *after)
    if split:
        return results[0], results[1:]
    return results[0], [
        lax.dynamic_slice_in_dim(results[0], run_next[s] * share, share, 1) for s in range(runs)
    ]


def dense(left, right, out_type, right_transposed=False, after=()):
    rows, depth = left.shape
    width = right.shape[0] if right_transposed else right.shape[1]
    step = chunk_of(width // 128, 12) * 128
    out_shape = jax.ShapeDtypeStruct((rows, width), out_type)
    if right_transposed:
        right_spec = pl.BlockSpec((step, depth), lambda i: (i, 0))
    else:
        right_spec = pl.BlockSpec((depth, step), lambda i: (0, i))

    def kernel(left_ref, right_ref, *refs):
        product = (dot_nt if right_transposed else dot)(left_ref[...], right_ref[...])
        refs[-1][...] = product.astype(out_type)

    return pl.pallas_call(
        kernel,
        grid=(width // step,),
        in_specs=[whole((rows, depth)), right_spec] + [ANY] * len(after),
        out_specs=pl.BlockSpec((rows, step), lambda i: (0, i)),
        out_shape=out_shape,
        compiler_params=params(),
        name="dense_nt" if right_transposed else "dense",
        cost_estimate=cost(left, right, out_shape),
    )(left, right, *after)


def dense_added(left, right, base, right_transposed=False, after=()):
    rows, depth = left.shape
    width = base.shape[1]
    step = chunk_of(depth // 128, 12) * 128
    if right_transposed:
        right_spec = pl.BlockSpec((width, step), lambda i: (0, i))
    else:
        right_spec = pl.BlockSpec((step, width), lambda i: (i, 0))

    def kernel(left_ref, right_ref, base_ref, *refs):
        out_ref, total_ref = refs[-2], refs[-1]
        here = pl.program_id(0)

        @pl.when(here == 0)
        def _():
            total_ref[...] = base_ref[...].astype(F32)

        total_ref[...] += (dot_nt if right_transposed else dot)(left_ref[...], right_ref[...])

        @pl.when(here == depth // step - 1)
        def _():
            out_ref[...] = total_ref[...].astype(out_ref.dtype)

    return pl.pallas_call(
        kernel,
        grid=(depth // step,),
        in_specs=[pl.BlockSpec((rows, step), lambda i: (0, i)), right_spec, whole(base.shape)]
        + [ANY] * len(after),
        out_specs=whole(base.shape),
        out_shape=jax.ShapeDtypeStruct(base.shape, base.dtype),
        scratch_shapes=[pltpu.VMEM(base.shape, F32)],
        compiler_params=params(),
        name="added_nt" if right_transposed else "added",
        cost_estimate=cost(left, right, base),
    )(left, right, base, *after)


def hidden_rows(up, gathered, run_rows, places, blocks, kept, part, rows, after=()):
    depth, width = up.shape
    tokens = gathered.shape[0]
    size = width // blocks
    chunk = chunk_of(blocks, 4)
    levels = places.shape[0]
    again = blocks - kept
    others = tokens - rows
    sent = [jax.ShapeDtypeStruct((kept * part, tokens), BF16)] * levels
    if again:
        sent += [jax.ShapeDtypeStruct((again * size, others), BF16)] * levels

    def kernel(run_ref, place_ref, up_ref, inputs_ref, *refs):
        whole_ref, out_ref, *sent_refs, full_ref = refs[len(after) :]
        full_ref[...] = dot(inputs_ref[...], up_ref[...]).astype(BF16).T
        for c in range(chunk):
            first = pl.multiple_of(run_ref[0] * part, part) + c * size
            for s in range(1, tokens // rows):
                there = pl.multiple_of(run_ref[s] * rows, rows)
                piece = full_ref[c * size : (c + 1) * size, pl.ds(there, rows)]
                whole_ref[c, :, (s - 1) * rows : s * rows] = piece
            out_ref[c] = full_ref[pl.ds(first, part), :]
            for lv in range(levels):
                place = place_ref[lv, pl.program_id(0) * chunk + c]

                if again:

                    @pl.when(place >= kept)
                    def _(place=place, lv=lv, c=c):
                        there = pl.multiple_of((place - kept) * size, size)
                        sent_refs[levels + lv][pl.ds(there, size), :] = whole_ref[c]

                @pl.when(place < kept)
                def _(place=place, lv=lv, c=c):
                    there = pl.multiple_of(place * part, part)
                    sent_refs[lv][pl.ds(there, part), :] = out_ref[c]

    return pl.pallas_call(
        kernel,
        grid_spec=pltpu.PrefetchScalarGridSpec(
            num_scalar_prefetch=2,
            grid=(blocks // chunk,),
            in_specs=[
                pl.BlockSpec((depth, chunk * size), lambda i, *_: (0, i)),
                column_half(tokens, depth, 0),
            ]
            + [ANY] * len(after),
            out_specs=[
                pl.BlockSpec((chunk, size, others), lambda i, *_: (i, 0, 0)),
                pl.BlockSpec((chunk, part, tokens), lambda i, *_: (i, 0, 0)),
            ]
            + [whole(shape.shape) for shape in sent],
            scratch_shapes=[pltpu.VMEM((chunk * size, tokens), BF16)],
        ),
        out_shape=[
            jax.ShapeDtypeStruct((blocks, size, others), BF16),
            jax.ShapeDtypeStruct((blocks, part, tokens), BF16),
        ]
        + sent,
        compiler_params=params(),
        name="hidden_rows",
        cost_estimate=cost(up, jax.ShapeDtypeStruct((blocks, size, tokens), BF16)),
    )(run_rows, places, up, gathered, *after)


def down_first(activated, down, base, gathered, kept, after=()):
    rows, width = activated.shape
    features = down.shape[1]
    tokens = gathered.shape[0]
    step = chunk_of(math.gcd(width, kept) // 128, 8) * 128
    out_type = BF16 if kept == width else F32

    def kernel(act_ref, down_ref, base_ref, all_ref, *refs):
        out_ref, grad_ref, total_ref = refs[-3:]
        here = pl.program_id(0)

        @pl.when(here == 0)
        def _():
            total_ref[...] = base_ref[...].astype(F32)

        total_ref[...] += dot(act_ref[...], down_ref[...])
        grad_ref[...] = dot_nt(all_ref[...], down_ref[...]).astype(BF16)

        @pl.when(here == kept // step - 1)
        def _():
            out_ref[...] = total_ref[...].astype(out_type)

    out_shape = [
        jax.ShapeDtypeStruct((rows, features), out_type),
        jax.ShapeDtypeStruct((tokens, kept), BF16),
    ]
    return pl.pallas_call(
        kernel,
        grid=(kept // step,),
        in_specs=[
            pl.BlockSpec((rows, step), lambda i: (0, i)),
            pl.BlockSpec((step, features), lambda i: (i, 0)),
            whole((rows, features)),
            column_half(tokens, features, 1),
        ]
        + [ANY] * len(after),
        out_specs=[
            whole((rows, features)),
            pl.BlockSpec((tokens, step), lambda i: (0, i)),
        ],
        out_shape=out_shape,
        scratch_shapes=[pltpu.VMEM((rows, features), F32)],
        compiler_params=params(),
        name="down_first",
        cost_estimate=cost(activated, down, out_shape[1]),
    )(activated, down, base, gathered, *after)


def down_rest(activated, down, partial, gathered, run_rows, kept, after=()):
    rows, width = activated.shape
    features = down.shape[1]
    tokens = gathered.shape[0]
    others = tokens - rows
    step = chunk_of(math.gcd(width, kept) // 128, 8) * 128
    first = kept // step

    def kernel(run_ref, act_ref, down_ref, partial_ref, all_ref, *refs):
        out_ref, grad_ref, rest_ref, total_ref = refs[-4:]
        here = pl.program_id(0)

        @pl.when(here == 0)
        def _():
            total_ref[...] = partial_ref[...]
            for s in range(1, tokens // rows):
                there = pl.multiple_of(run_ref[s] * rows, rows)
                rest_ref[(s - 1) * rows : s * rows, :] = all_ref[pl.ds(there, rows), :]

        total_ref[...] += dot(act_ref[...], down_ref[...])
        grad_ref[...] = dot_nt(down_ref[...], rest_ref[...])

        @pl.when(here == width // step - first - 1)
        def _():
            out_ref[...] = total_ref[...].astype(BF16)

    out_shape = [
        jax.ShapeDtypeStruct((rows, features), BF16),
        jax.ShapeDtypeStruct((width - kept, others), F32),
        jax.ShapeDtypeStruct((others, features), BF16),
    ]
    return pl.pallas_call(
        kernel,
        grid_spec=pltpu.PrefetchScalarGridSpec(
            num_scalar_prefetch=1,
            grid=(width // step - first,),
            in_specs=[
                pl.BlockSpec((rows, step), lambda i, *_: (0, first + i)),
                pl.BlockSpec((step, features), lambda i, *_: (first + i, 0)),
                whole((rows, features)),
                column_half(tokens, features, 1),
            ]
            + [ANY] * len(after),
            out_specs=[
                whole((rows, features)),
                pl.BlockSpec((step, others), lambda i, *_: (i, 0)),
                whole((others, features)),
            ],
            scratch_shapes=[pltpu.VMEM((rows, features), F32)],
        ),
        out_shape=out_shape,
        compiler_params=params(),
        name="down_rest",
        cost_estimate=cost(out_shape[1], out_shape[1], partial, partial),
    )(run_rows, activated, down, partial, gathered, *after)


def mix_gradient(mixed_all, act_grad_all, hidden_part, received, perm, scale, made=None):
    tokens, width = mixed_all.shape
    blocks, part, _ = hidden_part.shape
    size = part * lax.axis_size("dp")
    kept = width // size
    chunk = chunk_of(kept, 4)
    count = 2 + len(received)
    given = whole((kept * part, tokens))

    def kernel(perm_ref, mixed_ref, grad_ref, part_ref, *refs):
        given_refs, out_ref = refs[: len(received)], refs[-1]
        step = pl.program_id(0)
        for c in range(chunk):
            here = slice(c * size, (c + 1) * size)
            block = step * chunk + c
            slope = gelu_slope(mixed_ref[:, here].astype(F32))
            delta = (grad_ref[:, here].astype(F32) * slope).astype(BF16)
            rows = pl.ds(pl.multiple_of(block * part, part), part)
            picked = jnp.concatenate(
                [part_ref[block], part_ref[perm_ref[block]]] + [ref[rows, :] for ref in given_refs],
                axis=0,
            )
            result = dot(picked, delta) * scale
            for k in range(count):
                out_ref[k, c] = result[k * part : (k + 1) * part]

    columns = pl.BlockSpec((tokens, chunk * size), lambda i, *_: (0, i))
    return pl.pallas_call(
        kernel,
        grid_spec=pltpu.PrefetchScalarGridSpec(
            num_scalar_prefetch=1,
            grid=(kept // chunk,),
            in_specs=[columns, columns, whole(hidden_part.shape)]
            + [given] * len(received)
            + ([] if made is None else [ANY]),
            out_specs=pl.BlockSpec((count, chunk, part, size), lambda i, *_: (0, i, 0, 0)),
        ),
        out_shape=jax.ShapeDtypeStruct((count, blocks, part, size), F32),
        input_output_aliases={} if made is None else {4 + len(received): 0},
        compiler_params=params(),
        name="mix_gradient",
        cost_estimate=cost(mixed_all, act_grad_all),
    )(perm, mixed_all, act_grad_all, hidden_part, *received, *([] if made is None else [made]))


def recomputed(
    own_sources, own_delta, others, received, index, act_grad_rest, run, mix_weight, scale, after=()
):
    blocks, size, tokens = others.shape
    rows = own_delta.shape[0]
    count = mix_weight.shape[0]
    again = act_grad_rest.shape[0] // size
    kept = blocks - again
    part = size // lax.axis_size("dp")
    chunk = chunk_of(math.gcd(again, kept), 2)

    def kernel(index_ref, run_ref, *refs):
        straight_ref, *refs = refs
        permuted_refs, refs = refs[:chunk], refs[chunk:]
        received_refs, refs = refs[: len(received)], refs[len(received) :]
        own_refs, refs = refs[: count * chunk], refs[count * chunk :]
        weight_refs, refs = refs[:count], refs[count:]
        grad_ref, delta_ref = refs[:2]
        out_ref, act_ref, full_ref = refs[-3:]
        first = pl.multiple_of(run_ref[0] * part, part)
        for c in range(chunk):
            here = pl.ds(c * size, size)
            sources = [straight_ref.at[c], permuted_refs[c].at[0]]
            sources += [ref.at[here] for ref in received_refs]
            mixed = None
            for k in range(count):
                term = dot_tn(weight_refs[k][0, c], sources[k][...])
                mixed = term if mixed is None else mixed + term
                full_ref[c * count + k] = dot_tn(own_refs[k * chunk + c][...], delta_ref[:, here])
            act_ref[c] = gelu_tanh(mixed).astype(BF16)
            delta = (grad_ref[here, :] * gelu_slope(mixed)).astype(BF16)
            picked = jnp.concatenate([ref[pl.ds(first, part), :] for ref in sources], axis=0)
            result = dot_nt(picked, delta)
            for k in range(count):
                own = full_ref[c * count + k, pl.ds(first, part), :]
                out_ref[k, c] = (result[k * part : (k + 1) * part] + own) * scale

    source_specs = [
        pl.BlockSpec((chunk, size, tokens), lambda i, *_: (kept // chunk + i, 0, 0))
    ]
    for c in range(chunk):
        source_specs.append(
            pl.BlockSpec(
                (1, size, tokens),
                functools.partial(lambda c, i, index, run: (index[1, kept + i * chunk + c], 0, 0), c),
            )
        )
    source_specs += [pl.BlockSpec((chunk * size, tokens), lambda i, *_: (i, 0))] * len(received)
    own_specs = [
        pl.BlockSpec(
            (rows, size),
            functools.partial(
                lambda k, c, i, index, run: (0, index[k, kept + i * chunk + c]), k, c
            ),
        )
        for k in range(count)
        for c in range(chunk)
    ]
    level_specs = [
        pl.BlockSpec(
            (1, chunk, size, size),
            functools.partial(lambda k, i, *_: (k, kept // chunk + i, 0, 0), k),
        )
        for k in range(count)
    ]
    return pl.pallas_call(
        kernel,
        grid_spec=pltpu.PrefetchScalarGridSpec(
            num_scalar_prefetch=2,
            grid=(again // chunk,),
            in_specs=source_specs
            + own_specs
            + level_specs
            + [
                pl.BlockSpec((chunk * size, tokens), lambda i, *_: (i, 0)),
                pl.BlockSpec((rows, chunk * size), lambda i, *_: (0, kept // chunk + i)),
            ]
            + [ANY] * len(after),
            out_specs=[
                pl.BlockSpec((count, chunk, part, size), lambda i, *_: (0, kept // chunk + i, 0, 0)),
                pl.BlockSpec((chunk, size, tokens), lambda i, *_: (i, 0, 0)),
            ],
            scratch_shapes=[pltpu.VMEM((chunk * count, size, size), F32)],
        ),
        out_shape=[
            jax.ShapeDtypeStruct((count, blocks, part, size), F32),
            jax.ShapeDtypeStruct((again, size, tokens), BF16),
        ],
        compiler_params=params(),
        name="recomputed",
        cost_estimate=cost(*received, *received, act_grad_rest),
    )(
        index, run, others, *([others] * chunk), *received,
        *[source for source in own_sources for _ in range(chunk)], *([mix_weight] * count),
        act_grad_rest, own_delta, *after,
    )


def up_gradient(gathered, height, pieces, run_rows, scale, after=()):
    tokens = gathered.shape[0]
    rows, width = pieces[0].shape
    runs = len(pieces)
    step = chunk_of(height // 128, 4) * 128

    def kernel(run_ref, inputs_ref, *refs):
        out_ref, all_ref = refs[-2:]

        @pl.when(pl.program_id(0) == 0)
        def _():
            for s in range(runs):
                first = pl.multiple_of(run_ref[s] * rows, rows)
                all_ref[pl.ds(first, rows), :] = refs[s][...]

        out_ref[...] = dot_tn(inputs_ref[...], all_ref[...]) * scale

    return pl.pallas_call(
        kernel,
        grid_spec=pltpu.PrefetchScalarGridSpec(
            num_scalar_prefetch=1,
            grid=(height // step,),
            in_specs=[pl.BlockSpec((tokens, step), lambda i, *_: (0, i))]
            + [whole((rows, width))] * runs
            + [ANY] * len(after),
            out_specs=pl.BlockSpec((step, width), lambda i, *_: (i, 0)),
            scratch_shapes=[pltpu.VMEM((tokens, width), BF16)],
        ),
        out_shape=jax.ShapeDtypeStruct((height, width), F32),
        compiler_params=params(),
        name="up_gradient",
        cost_estimate=cost(gathered, jax.ShapeDtypeStruct((height, width), F32)),
    )(run_rows, gathered, *pieces, *after)


def down_gradient(mixed_all, gathered, run, share, scale, after=()):
    tokens, width = gathered.shape[0], gathered.shape[1] // 2
    if share % 128 == 0:
        step = chunk_of(share // 128, 4) * 128
        first = run * (share // step)
    else:
        mixed_all = lax.dynamic_slice_in_dim(mixed_all, run * share, share, 1)
        step, first = share, run * 0

    def kernel(first_ref, mixed_ref, right_ref, *refs):
        activated = gelu_tanh(mixed_ref[...].astype(F32)).astype(BF16)
        refs[-1][...] = dot_tn(activated, right_ref[...]) * scale

    return pl.pallas_call(
        kernel,
        grid_spec=pltpu.PrefetchScalarGridSpec(
            num_scalar_prefetch=1,
            grid=(share // step,),
            in_specs=[
                pl.BlockSpec((tokens, step), lambda i, first: (0, first[0] + i)),
                column_half(tokens, width, 1),
            ]
            + [ANY] * len(after),
            out_specs=pl.BlockSpec((step, width), lambda i, *_: (i, 0)),
        ),
        out_shape=jax.ShapeDtypeStruct((share, width), F32),
        compiler_params=params(),
        name="down_gradient",
        cost_estimate=cost(gathered, jax.ShapeDtypeStruct((share, width), F32)),
    )(first[None], mixed_all, gathered, *after)


def down_gradient_split(
    mixed_all, act_rest, activated, gathered, own, rest, run, share, scale, after=()
):
    tokens, width = gathered.shape[0], gathered.shape[1] // 2
    again, size, others = act_rest.shape
    rows, kept = activated.shape[0], mixed_all.shape[1] // size
    count = share // size

    def kernel(run_ref, mixed_ref, act_ref, own_act_ref, right_ref, own_ref, rest_ref, *refs):
        out_ref = refs[-1]
        block = run_ref[0] * count + pl.program_id(0)

        @pl.when(block < kept)
        def _():
            act = gelu_tanh(mixed_ref[...].astype(F32)).astype(BF16)
            out_ref[...] = dot_tn(act, right_ref[...]) * scale

        @pl.when(block >= kept)
        def _():
            total = dot(act_ref[0], rest_ref[...]) + dot_tn(own_act_ref[...], own_ref[...])
            out_ref[...] = total * scale

    return pl.pallas_call(
        kernel,
        grid_spec=pltpu.PrefetchScalarGridSpec(
            num_scalar_prefetch=1,
            grid=(count,),
            in_specs=[
                pl.BlockSpec(
                    (tokens, size), lambda i, run: (0, jnp.minimum(run[0] * count + i, kept - 1))
                ),
                pl.BlockSpec(
                    (1, size, others),
                    lambda i, run: (jnp.clip(run[0] * count + i - kept, 0, again - 1), 0, 0),
                ),
                pl.BlockSpec((rows, size), lambda i, run: (0, run[0] * count + i)),
                column_half(tokens, width, 1),
                whole((rows, width)),
                whole((others, width)),
            ]
            + [ANY] * len(after),
            out_specs=pl.BlockSpec((size, width), lambda i, *_: (i, 0)),
        ),
        out_shape=jax.ShapeDtypeStruct((share, width), F32),
        compiler_params=params(),
        name="down_gradient_split",
        cost_estimate=cost(gathered, jax.ShapeDtypeStruct((share, width), F32)),
    )(run, mixed_all, act_rest, activated, gathered, own, rest, *after)


def held(values, after):
    count = len(values)
    return pl.pallas_call(
        lambda *refs: None,
        in_specs=[ANY] * (count + len(after)),
        out_specs=[ANY] * count,
        out_shape=[jax.ShapeDtypeStruct(v.shape, v.dtype) for v in values],
        input_output_aliases={k: k for k in range(count)},
        compiler_params=pltpu.CompilerParams(has_side_effects=True),
        name="held",
    )(*values, *after)


def body(inputs, out_grad, up_weight, mix_weight, output_factor_matrix, partner, local_perm):
    rows = inputs.shape[0]
    blocks, size = mix_weight.shape[1], mix_weight.shape[2]
    levels = partner.shape[0]
    up, down = up_weight[0], output_factor_matrix[0]
    width = up.shape[1]
    runs = lax.axis_size("dp")
    me, run = lax.axis_index("mp"), lax.axis_index("dp")
    base = me * blocks
    scale = (rows * runs) ** (-0.5)
    run_rows = ((run - jnp.arange(runs, dtype=jnp.int32)) % runs).astype(jnp.int32)
    perm_here = lax.dynamic_slice_in_dim(local_perm, base, blocks, 0) - base
    far_here = lax.dynamic_slice_in_dim(partner, base, blocks, 1)
    far_base = jnp.stack([jnp.bitwise_xor(me, 1 << lv) * blocks for lv in range(levels)])
    far_index = far_here - far_base[:, None]
    index = jnp.concatenate(
        [jnp.arange(blocks, dtype=jnp.int32)[None], perm_here[None], far_index], axis=0
    )
    which = [0, 0] + list(range(1, levels + 1))
    last = levels + 1
    part, share = size // runs, width // runs

    again = blocks // 3 if share % size == 0 else 0
    kept = blocks - again
    theirs = jnp.stack(
        [
            lax.dynamic_slice_in_dim(partner[lv], far_base[lv], blocks, 0) - base
            for lv in range(levels)
        ]
    )

    order = jnp.arange(blocks, dtype=jnp.int32)
    places = jnp.sum(
        jnp.where(theirs[:, None, :] == order[None, :, None], order[None, None, :], 0),
        axis=2,
        dtype=jnp.int32,
    )

    gathered = lax.all_gather(
        jnp.concatenate([inputs, out_grad], axis=1), "dp", axis=0, tiled=True
    )
    hidden = dense(inputs, up, BF16)
    received = [from_partner(hidden, "mp", lv) for lv in range(levels)]
    act_grad = dense(out_grad, down, F32, True, after=received[:-1])
    near = mixed_near(
        [hidden] + received[:-1], which[:-1], index[:-1], list(range(last)), mix_weight,
        after=(act_grad,),
    )
    mixed, activated, delta = mixed_last(
        received[-1], index[-1], last, mix_weight, near, act_grad, kept
    )
    mixed_all = lax.all_gather(mixed, "dp", axis=0, tiled=True)
    far = far_terms(delta, far_index, list(range(2, levels + 2)), mix_weight)
    far_received = [from_partner(far[lv], "mp", lv) for lv in range(levels)]
    outputs, act_grad_all = down_first(
        activated, down, inputs, gathered, kept * size, after=far[:1]
    )
    others, hidden_part, *sent = hidden_rows(
        up, gathered, run_rows, places, blocks, kept, part, rows,
        after=[outputs] + far_received[:1],
    )
    sources = [from_partner(piece, "mp", k % levels) for k, piece in enumerate(sent)]
    part_sources, whole_sources = sources[:levels], sources[levels:]
    run_next = ((run + jnp.arange(runs, dtype=jnp.int32)) % runs).astype(jnp.int32)
    hidden_grad, to_send = back_pass(
        delta, perm_here, mix_weight, far_received, run_next, after=[hidden_part] + sources[::levels]
    )
    rest = None
    if again:
        outputs, *rest = down_rest(
            activated, down, outputs, gathered, run_rows, kept * size, after=(hidden_grad,)
        )
    input_grad = dense_added(hidden_grad, up, out_grad, True, after=(outputs,))
    to_send = [to_send[0]] + list(held(to_send[1:], (input_grad,)))
    hidden_grad_pieces = [to_send[0]] + [rotated(to_send[s], "dp", s) for s in range(1, runs)]
    made, act_rest = None, input_grad
    if again:
        made, act_rest = recomputed(
            [hidden, hidden] + received, delta, others, whole_sources, index, rest[0], run[None],
            mix_weight, scale, after=(input_grad,),
        )
    mix_grad = mix_gradient(
        mixed_all, act_grad_all, hidden_part, part_sources, perm_here, scale, made
    )
    if again:
        down_grad = down_gradient_split(
            mixed_all, act_rest, activated, gathered, out_grad, rest[1], run[None], share, scale,
            after=(mix_grad,),
        )
    else:
        down_grad = down_gradient(mixed_all, gathered, run, share, scale, after=(mix_grad,))
    up_grad = up_gradient(
        gathered, up.shape[0], hidden_grad_pieces, run_rows, scale, after=(down_grad,)
    )
    return (outputs, input_grad, up_grad[None], mix_grad, down_grad[None])


def solution(mesh):
    return jax.shard_map(
        body,
        mesh=mesh,
        in_specs=(
            P(("groups", "dp"), "mp"),
            P(("groups", "dp"), "mp"),
            P("mp", None, None),
            P(None, "mp", None, None),
            P("mp", None, None),
            P(),
            P(),
        ),
        out_specs=(
            P(("groups", "dp"), "mp"),
            P(("groups", "dp"), "mp"),
            P(("groups", "mp"), None, "dp"),
            P("groups", "mp", "dp", None),
            P(("groups", "mp"), "dp", None),
        ),
        check_vma=False,
    )
```

```python
import functools
import math

import jax
import jax.numpy as jnp
from jax import lax
from jax.experimental import pallas as pl
from jax.experimental.pallas import tpu as pltpu
from jax.sharding import PartitionSpec as P

F32 = jnp.float32
BF16 = jnp.bfloat16
VMEM_BYTES = 56 * 1024 * 1024
ANY = pl.BlockSpec(memory_space=pl.ANY)


def from_partner(value, axis, apart):
    mask = 2**apart
    pairs = [(source, source ^ mask) for source in range(lax.axis_size(axis))]
    return lax.ppermute(value, axis, pairs)


def rotated(value, axis, shift):
    size = lax.axis_size(axis)
    return lax.ppermute(value, axis, [(i, (i + shift) % size) for i in range(size)])


def gelu_tanh(values):
    inner = 0.7978845608028654 * (values + 0.044715 * values * values * values)
    return 0.5 * values * (1.0 + jnp.tanh(inner))


def gelu_slope(values):
    inner = 0.7978845608028654 * (values + 0.044715 * values * values * values)
    tangent = jnp.tanh(inner)
    return 0.5 * (1.0 + tangent) + 0.5 * values * (1.0 - tangent * tangent) * 0.7978845608028654 * (
        1.0 + 3.0 * 0.044715 * values * values
    )


def dot(a, b):
    return jnp.dot(a, b, preferred_element_type=F32)


def dot_nt(a, b):
    return lax.dot_general(a, b, (((1,), (1,)), ((), ())), preferred_element_type=F32)


def dot_tn(a, b):
    return lax.dot_general(a, b, (((0,), (0,)), ((), ())), preferred_element_type=F32)


def params():
    return pltpu.CompilerParams(vmem_limit_bytes=VMEM_BYTES)


def cost(*arrays):
    moved = sum(math.prod(a.shape) * a.dtype.itemsize for a in arrays)
    return pl.CostEstimate(flops=0, bytes_accessed=int(2.2 * moved), transcendentals=0)


def level_shape(mix_weight):
    return jax.ShapeDtypeStruct(mix_weight.shape[1:], mix_weight.dtype)


def chunk_of(block_count, most):
    return max(c for c in range(1, most + 1) if block_count % c == 0)


def lanes(index, size):
    return pl.ds(pl.multiple_of(index * size, size), size)


def whole(shape):
    return pl.BlockSpec(shape, lambda i, *_: (0,) * len(shape))


def column_half(tokens, features, half):
    return pl.BlockSpec((tokens, features), lambda i, *_: (0, half))


def weight_specs(levels, chunk, size):
    return [
        pl.BlockSpec((1, chunk, size, size), functools.partial(lambda lv, i, *_: (lv, i, 0, 0), lv))
        for lv in levels
    ]


def mixed_near(sources, which, index, levels, mix_weight, after=()):
    rows, width = sources[0].shape
    blocks, size = mix_weight.shape[1], mix_weight.shape[2]
    chunk = chunk_of(blocks, 8)
    count = len(levels)
    near_shape = jax.ShapeDtypeStruct((rows, width), F32)

    def kernel(index_ref, *refs):
        source_refs, weight_refs, out_ref = refs[: len(sources)], refs[len(sources) :], refs[-1]
        step = pl.program_id(0)
        for c in range(chunk):
            total = None
            for k in range(count):
                picked = source_refs[which[k]][:, lanes(index_ref[k, step * chunk + c], size)]
                term = dot(picked, weight_refs[k][0, c])
                total = term if total is None else total + term
            out_ref[:, c * size : (c + 1) * size] = total

    return pl.pallas_call(
        kernel,
        grid_spec=pltpu.PrefetchScalarGridSpec(
            num_scalar_prefetch=1,
            grid=(blocks // chunk,),
            in_specs=[whole((rows, width)) for _ in sources]
            + weight_specs(levels, chunk, size)
            + [ANY] * len(after),
            out_specs=pl.BlockSpec((rows, chunk * size), lambda i, *_: (0, i)),
        ),
        out_shape=near_shape,
        compiler_params=params(),
        name="mixed_near",
        cost_estimate=cost(*sources, *[level_shape(mix_weight)] * count, near_shape),
    )(index, *sources, *([mix_weight] * count), *after)


def mixed_last(source, index, level, mix_weight, near, act_grad, kept, after=()):
    rows, width = source.shape
    blocks, size = mix_weight.shape[1], mix_weight.shape[2]
    chunk = chunk_of(math.gcd(blocks, kept), 8)

    def kernel(index_ref, source_ref, weight_ref, near_ref, grad_ref, *refs):
        mixed_ref, act_ref, delta_ref = refs[-3:]
        step = pl.program_id(0)
        for c in range(chunk):
            here = slice(c * size, (c + 1) * size)
            picked = source_ref[:, lanes(index_ref[step * chunk + c], size)]
            total = near_ref[:, here] + dot(picked, weight_ref[0, c])

            @pl.when(step < kept // chunk)
            def _(total=total, here=here):
                mixed_ref[:, here] = total.astype(BF16)

            act_ref[:, here] = gelu_tanh(total).astype(BF16)
            delta_ref[:, here] = (grad_ref[:, here] * gelu_slope(total)).astype(BF16)

    columns = pl.BlockSpec((rows, chunk * size), lambda i, *_: (0, i))
    return pl.pallas_call(
        kernel,
        grid_spec=pltpu.PrefetchScalarGridSpec(
            num_scalar_prefetch=1,
            grid=(blocks // chunk,),
            in_specs=[whole((rows, width))] + weight_specs([level], chunk, size)
            + [columns, columns]
            + [ANY] * len(after),
            out_specs=[
                pl.BlockSpec((rows, chunk * size), lambda i, *_: (0, jnp.minimum(i, kept // chunk - 1))),
                columns,
                columns,
            ],
        ),
        out_shape=[jax.ShapeDtypeStruct((rows, kept * size), BF16)]
        + [jax.ShapeDtypeStruct((rows, width), BF16)] * 2,
        compiler_params=params(),
        name="mixed_last",
        cost_estimate=cost(source, level_shape(mix_weight), near, act_grad, source, source),
    )(index, source, mix_weight, near, act_grad, *after)


def far_terms(delta, targets, levels, mix_weight, after=()):
    rows, width = delta.shape
    blocks, size = mix_weight.shape[1], mix_weight.shape[2]
    chunk = chunk_of(blocks, 8)
    count = len(levels)

    def kernel(target_ref, delta_ref, *refs):
        step = pl.program_id(0)
        for c in range(chunk):
            here = delta_ref[:, c * size : (c + 1) * size]
            for k in range(count):
                place = lanes(target_ref[k, step * chunk + c], size)
                refs[count + len(after) + k][:, place] = dot_nt(here, refs[k][0, c]).astype(BF16)

    return pl.pallas_call(
        kernel,
        grid_spec=pltpu.PrefetchScalarGridSpec(
            num_scalar_prefetch=1,
            grid=(blocks // chunk,),
            in_specs=[pl.BlockSpec((rows, chunk * size), lambda i, *_: (0, i))]
            + weight_specs(levels, chunk, size)
            + [ANY] * len(after),
            out_specs=[whole((rows, width))] * count,
        ),
        out_shape=[jax.ShapeDtypeStruct((rows, width), BF16)] * count,
        compiler_params=params(),
        name="far_terms",
        cost_estimate=cost(delta, *[level_shape(mix_weight), delta] * count),
    )(targets, delta, *([mix_weight] * count), *after)


def back_pass(delta, perm, mix_weight, terms, run_next, after=()):
    rows, width = delta.shape
    blocks, size = mix_weight.shape[1], mix_weight.shape[2]
    chunk = chunk_of(blocks, 8)
    runs = run_next.shape[0]
    share = width // runs
    split = share % 128 == 0

    def kernel(perm_ref, run_ref, delta_ref, own_ref, perm_weight_ref, *refs):
        out_ref, *piece_refs, total_ref = refs[len(terms) + len(after) :]
        step = pl.program_id(0)

        @pl.when(step == 0)
        def _():
            total = refs[0][...].astype(F32)
            for term_ref in refs[1 : len(terms)]:
                total = total + term_ref[...].astype(F32)
            total_ref[...] = total

        for c in range(chunk):
            here = delta_ref[:, c * size : (c + 1) * size]
            total_ref[:, lanes(step * chunk + c, size)] += dot_nt(here, own_ref[0, c])
            total_ref[:, lanes(perm_ref[step * chunk + c], size)] += dot_nt(here, perm_weight_ref[0, c])

        @pl.when(step == blocks // chunk - 1)
        def _():
            out_ref[...] = total_ref[...].astype(BF16)
            for s, piece_ref in enumerate(piece_refs):
                piece_ref[...] = total_ref[:, lanes(run_ref[s], share)].astype(BF16)

    results = pl.pallas_call(
        kernel,
        grid_spec=pltpu.PrefetchScalarGridSpec(
            num_scalar_prefetch=2,
            grid=(blocks // chunk,),
            in_specs=[pl.BlockSpec((rows, chunk * size), lambda i, *_: (0, i))]
            + weight_specs([0, 1], chunk, size)
            + [whole((rows, width))] * len(terms)
            + [ANY] * len(after),
            out_specs=[whole((rows, width))] + [whole((rows, share))] * (runs if split else 0),
            scratch_shapes=[pltpu.VMEM((rows, width), F32)],
        ),
        out_shape=[jax.ShapeDtypeStruct((rows, width), BF16)]
        + [jax.ShapeDtypeStruct((rows, share), BF16)] * (runs if split else 0),
        compiler_params=params(),
        name="back_pass",
        cost_estimate=cost(delta, *terms, *[level_shape(mix_weight)] * 2),
    )(perm, run_next, delta, mix_weight, mix_weight, *terms, *after)
    if split:
        return results[0], results[1:]
    return results[0], [
        lax.dynamic_slice_in_dim(results[0], run_next[s] * share, share, 1) for s in range(runs)
    ]


def dense(left, right, out_type, right_transposed=False, after=()):
    rows, depth = left.shape
    width = right.shape[0] if right_transposed else right.shape[1]
    step = chunk_of(width // 128, 12) * 128
    out_shape = jax.ShapeDtypeStruct((rows, width), out_type)
    if right_transposed:
        right_spec = pl.BlockSpec((step, depth), lambda i: (i, 0))
    else:
        right_spec = pl.BlockSpec((depth, step), lambda i: (0, i))

    def kernel(left_ref, right_ref, *refs):
        product = (dot_nt if right_transposed else dot)(left_ref[...], right_ref[...])
        refs[-1][...] = product.astype(out_type)

    return pl.pallas_call(
        kernel,
        grid=(width // step,),
        in_specs=[whole((rows, depth)), right_spec] + [ANY] * len(after),
        out_specs=pl.BlockSpec((rows, step), lambda i: (0, i)),
        out_shape=out_shape,
        compiler_params=params(),
        name="dense_nt" if right_transposed else "dense",
        cost_estimate=cost(left, right, out_shape),
    )(left, right, *after)


def dense_added(left, right, base, right_transposed=False, after=()):
    rows, depth = left.shape
    width = base.shape[1]
    step = chunk_of(depth // 128, 12) * 128
    if right_transposed:
        right_spec = pl.BlockSpec((width, step), lambda i: (0, i))
    else:
        right_spec = pl.BlockSpec((step, width), lambda i: (i, 0))

    def kernel(left_ref, right_ref, base_ref, *refs):
        out_ref, total_ref = refs[-2], refs[-1]
        here = pl.program_id(0)

        @pl.when(here == 0)
        def _():
            total_ref[...] = base_ref[...].astype(F32)

        total_ref[...] += (dot_nt if right_transposed else dot)(left_ref[...], right_ref[...])

        @pl.when(here == depth // step - 1)
        def _():
            out_ref[...] = total_ref[...].astype(out_ref.dtype)

    return pl.pallas_call(
        kernel,
        grid=(depth // step,),
        in_specs=[pl.BlockSpec((rows, step), lambda i: (0, i)), right_spec, whole(base.shape)]
        + [ANY] * len(after),
        out_specs=whole(base.shape),
        out_shape=jax.ShapeDtypeStruct(base.shape, base.dtype),
        scratch_shapes=[pltpu.VMEM(base.shape, F32)],
        compiler_params=params(),
        name="added_nt" if right_transposed else "added",
        cost_estimate=cost(left, right, base),
    )(left, right, base, *after)


def hidden_rows(up, gathered, run_rows, places, blocks, kept, part, rows, after=()):
    depth, width = up.shape
    tokens = gathered.shape[0]
    size = width // blocks
    chunk = chunk_of(blocks, 6)
    levels = places.shape[0]
    again = blocks - kept
    others = tokens - rows
    sent = [jax.ShapeDtypeStruct((kept * part, tokens), BF16)] * levels
    if again:
        sent += [jax.ShapeDtypeStruct((again * size, others), BF16)] * levels

    def kernel(run_ref, place_ref, up_ref, inputs_ref, *refs):
        whole_ref, out_ref, *sent_refs, full_ref = refs[len(after) :]
        full_ref[...] = dot(inputs_ref[...], up_ref[...]).astype(BF16).T
        for c in range(chunk):
            first = pl.multiple_of(run_ref[0] * part, part) + c * size
            for s in range(1, tokens // rows):
                there = pl.multiple_of(run_ref[s] * rows, rows)
                piece = full_ref[c * size : (c + 1) * size, pl.ds(there, rows)]
                whole_ref[c, :, (s - 1) * rows : s * rows] = piece
            out_ref[c] = full_ref[pl.ds(first, part), :]
            for lv in range(levels):
                place = place_ref[lv, pl.program_id(0) * chunk + c]

                if again:

                    @pl.when(place >= kept)
                    def _(place=place, lv=lv, c=c):
                        there = pl.multiple_of((place - kept) * size, size)
                        sent_refs[levels + lv][pl.ds(there, size), :] = whole_ref[c]

                @pl.when(place < kept)
                def _(place=place, lv=lv, c=c):
                    there = pl.multiple_of(place * part, part)
                    sent_refs[lv][pl.ds(there, part), :] = out_ref[c]

    return pl.pallas_call(
        kernel,
        grid_spec=pltpu.PrefetchScalarGridSpec(
            num_scalar_prefetch=2,
            grid=(blocks // chunk,),
            in_specs=[
                pl.BlockSpec((depth, chunk * size), lambda i, *_: (0, i)),
                column_half(tokens, depth, 0),
            ]
            + [ANY] * len(after),
            out_specs=[
                pl.BlockSpec((chunk, size, others), lambda i, *_: (i, 0, 0)),
                pl.BlockSpec((chunk, part, tokens), lambda i, *_: (i, 0, 0)),
            ]
            + [whole(shape.shape) for shape in sent],
            scratch_shapes=[pltpu.VMEM((chunk * size, tokens), BF16)],
        ),
        out_shape=[
            jax.ShapeDtypeStruct((blocks, size, others), BF16),
            jax.ShapeDtypeStruct((blocks, part, tokens), BF16),
        ]
        + sent,
        compiler_params=params(),
        name="hidden_rows",
        cost_estimate=cost(up, jax.ShapeDtypeStruct((blocks, size, tokens), BF16)),
    )(run_rows, places, up, gathered, *after)


def down_first(activated, down, base, gathered, kept, after=()):
    rows, width = activated.shape
    features = down.shape[1]
    tokens = gathered.shape[0]
    step = chunk_of(math.gcd(width, kept) // 128, 8) * 128
    out_type = BF16 if kept == width else F32

    def kernel(act_ref, down_ref, base_ref, all_ref, *refs):
        out_ref, grad_ref, total_ref = refs[-3:]
        here = pl.program_id(0)

        @pl.when(here == 0)
        def _():
            total_ref[...] = base_ref[...].astype(F32)

        total_ref[...] += dot(act_ref[...], down_ref[...])
        grad_ref[...] = dot_nt(all_ref[...], down_ref[...]).astype(BF16)

        @pl.when(here == kept // step - 1)
        def _():
            out_ref[...] = total_ref[...].astype(out_type)

    out_shape = [
        jax.ShapeDtypeStruct((rows, features), out_type),
        jax.ShapeDtypeStruct((tokens, kept), BF16),
    ]
    return pl.pallas_call(
        kernel,
        grid=(kept // step,),
        in_specs=[
            pl.BlockSpec((rows, step), lambda i: (0, i)),
            pl.BlockSpec((step, features), lambda i: (i, 0)),
            whole((rows, features)),
            column_half(tokens, features, 1),
        ]
        + [ANY] * len(after),
        out_specs=[
            whole((rows, features)),
            pl.BlockSpec((tokens, step), lambda i: (0, i)),
        ],
        out_shape=out_shape,
        scratch_shapes=[pltpu.VMEM((rows, features), F32)],
        compiler_params=params(),
        name="down_first",
        cost_estimate=cost(activated, down, out_shape[1]),
    )(activated, down, base, gathered, *after)


def down_rest(activated, down, partial, gathered, run_rows, kept, after=()):
    rows, width = activated.shape
    features = down.shape[1]
    tokens = gathered.shape[0]
    others = tokens - rows
    step = chunk_of(math.gcd(width, kept) // 128, 8) * 128
    first = kept // step

    def kernel(run_ref, act_ref, down_ref, partial_ref, all_ref, *refs):
        out_ref, grad_ref, rest_ref, total_ref = refs[-4:]
        here = pl.program_id(0)

        @pl.when(here == 0)
        def _():
            total_ref[...] = partial_ref[...]
            for s in range(1, tokens // rows):
                there = pl.multiple_of(run_ref[s] * rows, rows)
                rest_ref[(s - 1) * rows : s * rows, :] = all_ref[pl.ds(there, rows), :]

        total_ref[...] += dot(act_ref[...], down_ref[...])
        grad_ref[...] = dot_nt(down_ref[...], rest_ref[...])

        @pl.when(here == width // step - first - 1)
        def _():
            out_ref[...] = total_ref[...].astype(BF16)

    out_shape = [
        jax.ShapeDtypeStruct((rows, features), BF16),
        jax.ShapeDtypeStruct((width - kept, others), F32),
        jax.ShapeDtypeStruct((others, features), BF16),
    ]
    return pl.pallas_call(
        kernel,
        grid_spec=pltpu.PrefetchScalarGridSpec(
            num_scalar_prefetch=1,
            grid=(width // step - first,),
            in_specs=[
                pl.BlockSpec((rows, step), lambda i, *_: (0, first + i)),
                pl.BlockSpec((step, features), lambda i, *_: (first + i, 0)),
                whole((rows, features)),
                column_half(tokens, features, 1),
            ]
            + [ANY] * len(after),
            out_specs=[
                whole((rows, features)),
                pl.BlockSpec((step, others), lambda i, *_: (i, 0)),
                whole((others, features)),
            ],
            scratch_shapes=[pltpu.VMEM((rows, features), F32)],
        ),
        out_shape=out_shape,
        compiler_params=params(),
        name="down_rest",
        cost_estimate=cost(out_shape[1], out_shape[1], partial, partial),
    )(run_rows, activated, down, partial, gathered, *after)


def mix_gradient(mixed_all, act_grad_all, hidden_part, received, perm, scale, made=None, after=()):
    tokens, width = mixed_all.shape
    blocks, part, _ = hidden_part.shape
    size = part * lax.axis_size("dp")
    kept = width // size
    chunk = chunk_of(kept, 4)
    count = 2 + len(received)
    given = whole((kept * part, tokens))

    def kernel(perm_ref, mixed_ref, grad_ref, part_ref, *refs):
        given_refs, out_ref = refs[: len(received)], refs[-1]
        step = pl.program_id(0)
        for c in range(chunk):
            here = slice(c * size, (c + 1) * size)
            block = step * chunk + c
            slope = gelu_slope(mixed_ref[:, here].astype(F32))
            delta = (grad_ref[:, here].astype(F32) * slope).astype(BF16)
            rows = pl.ds(pl.multiple_of(block * part, part), part)
            picked = jnp.concatenate(
                [part_ref[block], part_ref[perm_ref[block]]] + [ref[rows, :] for ref in given_refs],
                axis=0,
            )
            result = dot(picked, delta) * scale
            for k in range(count):
                out_ref[k, c] = result[k * part : (k + 1) * part]

    columns = pl.BlockSpec((tokens, chunk * size), lambda i, *_: (0, i))
    return pl.pallas_call(
        kernel,
        grid_spec=pltpu.PrefetchScalarGridSpec(
            num_scalar_prefetch=1,
            grid=(kept // chunk,),
            in_specs=[columns, columns, whole(hidden_part.shape)]
            + [given] * len(received)
            + ([] if made is None else [ANY])
            + [ANY] * len(after),
            out_specs=pl.BlockSpec((count, chunk, part, size), lambda i, *_: (0, i, 0, 0)),
        ),
        out_shape=jax.ShapeDtypeStruct((count, blocks, part, size), F32),
        input_output_aliases={} if made is None else {4 + len(received): 0},
        compiler_params=params(),
        name="mix_gradient",
        cost_estimate=cost(mixed_all, act_grad_all),
    )(perm, mixed_all, act_grad_all, hidden_part, *received, *([] if made is None else [made]), *after)


def recomputed(
    own_sources, own_delta, others, received, index, act_grad_rest, run, mix_weight, scale, after=()
):
    blocks, size, tokens = others.shape
    rows = own_delta.shape[0]
    count = mix_weight.shape[0]
    again = act_grad_rest.shape[0] // size
    kept = blocks - again
    part = size // lax.axis_size("dp")
    chunk = chunk_of(math.gcd(again, kept), 2)

    def kernel(index_ref, run_ref, *refs):
        straight_ref, *refs = refs
        permuted_refs, refs = refs[:chunk], refs[chunk:]
        received_refs, refs = refs[: len(received)], refs[len(received) :]
        own_refs, refs = refs[: count * chunk], refs[count * chunk :]
        weight_refs, refs = refs[:count], refs[count:]
        grad_ref, delta_ref = refs[:2]
        out_ref, act_ref, full_ref = refs[-3:]
        first = pl.multiple_of(run_ref[0] * part, part)
        for c in range(chunk):
            here = pl.ds(c * size, size)
            sources = [straight_ref.at[c], permuted_refs[c].at[0]]
            sources += [ref.at[here] for ref in received_refs]
            mixed = None
            for k in range(count):
                term = dot_tn(weight_refs[k][0, c], sources[k][...])
                mixed = term if mixed is None else mixed + term
                full_ref[c * count + k] = dot_tn(own_refs[k * chunk + c][...], delta_ref[:, here])
            act_ref[c] = gelu_tanh(mixed).astype(BF16)
            delta = (grad_ref[here, :] * gelu_slope(mixed)).astype(BF16)
            picked = jnp.concatenate([ref[pl.ds(first, part), :] for ref in sources], axis=0)
            result = dot_nt(picked, delta)
            for k in range(count):
                own = full_ref[c * count + k, pl.ds(first, part), :]
                out_ref[k, c] = (result[k * part : (k + 1) * part] + own) * scale

    source_specs = [
        pl.BlockSpec((chunk, size, tokens), lambda i, *_: (kept // chunk + i, 0, 0))
    ]
    for c in range(chunk):
        source_specs.append(
            pl.BlockSpec(
                (1, size, tokens),
                functools.partial(lambda c, i, index, run: (index[1, kept + i * chunk + c], 0, 0), c),
            )
        )
    source_specs += [pl.BlockSpec((chunk * size, tokens), lambda i, *_: (i, 0))] * len(received)
    own_specs = [
        pl.BlockSpec(
            (rows, size),
            functools.partial(
                lambda k, c, i, index, run: (0, index[k, kept + i * chunk + c]), k, c
            ),
        )
        for k in range(count)
        for c in range(chunk)
    ]
    level_specs = [
        pl.BlockSpec(
            (1, chunk, size, size),
            functools.partial(lambda k, i, *_: (k, kept // chunk + i, 0, 0), k),
        )
        for k in range(count)
    ]
    return pl.pallas_call(
        kernel,
        grid_spec=pltpu.PrefetchScalarGridSpec(
            num_scalar_prefetch=2,
            grid=(again // chunk,),
            in_specs=source_specs
            + own_specs
            + level_specs
            + [
                pl.BlockSpec((chunk * size, tokens), lambda i, *_: (i, 0)),
                pl.BlockSpec((rows, chunk * size), lambda i, *_: (0, kept // chunk + i)),
            ]
            + [ANY] * len(after),
            out_specs=[
                pl.BlockSpec((count, chunk, part, size), lambda i, *_: (0, kept // chunk + i, 0, 0)),
                pl.BlockSpec((chunk, size, tokens), lambda i, *_: (i, 0, 0)),
            ],
            scratch_shapes=[pltpu.VMEM((chunk * count, size, size), F32)],
        ),
        out_shape=[
            jax.ShapeDtypeStruct((count, blocks, part, size), F32),
            jax.ShapeDtypeStruct((again, size, tokens), BF16),
        ],
        compiler_params=params(),
        name="recomputed",
        cost_estimate=cost(*received, *received, act_grad_rest),
    )(
        index, run, others, *([others] * chunk), *received,
        *[source for source in own_sources for _ in range(chunk)], *([mix_weight] * count),
        act_grad_rest, own_delta, *after,
    )


def up_gradient(gathered, height, pieces, run_rows, scale, after=()):
    tokens = gathered.shape[0]
    rows, width = pieces[0].shape
    runs = len(pieces)
    step = chunk_of(height // 128, 4) * 128

    def kernel(run_ref, inputs_ref, *refs):
        out_ref, all_ref = refs[-2:]

        @pl.when(pl.program_id(0) == 0)
        def _():
            for s in range(runs):
                first = pl.multiple_of(run_ref[s] * rows, rows)
                all_ref[pl.ds(first, rows), :] = refs[s][...]

        out_ref[...] = dot_tn(inputs_ref[...], all_ref[...]) * scale

    return pl.pallas_call(
        kernel,
        grid_spec=pltpu.PrefetchScalarGridSpec(
            num_scalar_prefetch=1,
            grid=(height // step,),
            in_specs=[pl.BlockSpec((tokens, step), lambda i, *_: (0, i))]
            + [whole((rows, width))] * runs
            + [ANY] * len(after),
            out_specs=pl.BlockSpec((step, width), lambda i, *_: (i, 0)),
            scratch_shapes=[pltpu.VMEM((tokens, width), BF16)],
        ),
        out_shape=jax.ShapeDtypeStruct((height, width), F32),
        compiler_params=params(),
        name="up_gradient",
        cost_estimate=cost(gathered, jax.ShapeDtypeStruct((height, width), F32)),
    )(run_rows, gathered, *pieces, *after)


def down_gradient(mixed_all, gathered, run, share, scale, after=()):
    tokens, width = gathered.shape[0], gathered.shape[1] // 2
    if share % 128 == 0:
        step = chunk_of(share // 128, 4) * 128
        first = run * (share // step)
    else:
        mixed_all = lax.dynamic_slice_in_dim(mixed_all, run * share, share, 1)
        step, first = share, run * 0

    def kernel(first_ref, mixed_ref, right_ref, *refs):
        activated = gelu_tanh(mixed_ref[...].astype(F32)).astype(BF16)
        refs[-1][...] = dot_tn(activated, right_ref[...]) * scale

    return pl.pallas_call(
        kernel,
        grid_spec=pltpu.PrefetchScalarGridSpec(
            num_scalar_prefetch=1,
            grid=(share // step,),
            in_specs=[
                pl.BlockSpec((tokens, step), lambda i, first: (0, first[0] + i)),
                column_half(tokens, width, 1),
            ]
            + [ANY] * len(after),
            out_specs=pl.BlockSpec((step, width), lambda i, *_: (i, 0)),
        ),
        out_shape=jax.ShapeDtypeStruct((share, width), F32),
        compiler_params=params(),
        name="down_gradient",
        cost_estimate=cost(gathered, jax.ShapeDtypeStruct((share, width), F32)),
    )(first[None], mixed_all, gathered, *after)


def down_gradient_split(
    mixed_all, act_rest, activated, gathered, own, rest, run, share, scale, after=()
):
    tokens, width = gathered.shape[0], gathered.shape[1] // 2
    again, size, others = act_rest.shape
    rows, kept = activated.shape[0], mixed_all.shape[1] // size
    count = share // size

    def kernel(run_ref, mixed_ref, act_ref, own_act_ref, right_ref, own_ref, rest_ref, *refs):
        out_ref = refs[-1]
        block = run_ref[0] * count + pl.program_id(0)

        @pl.when(block < kept)
        def _():
            act = gelu_tanh(mixed_ref[...].astype(F32)).astype(BF16)
            out_ref[...] = dot_tn(act, right_ref[...]) * scale

        @pl.when(block >= kept)
        def _():
            total = dot(act_ref[0], rest_ref[...]) + dot_tn(own_act_ref[...], own_ref[...])
            out_ref[...] = total * scale

    return pl.pallas_call(
        kernel,
        grid_spec=pltpu.PrefetchScalarGridSpec(
            num_scalar_prefetch=1,
            grid=(count,),
            in_specs=[
                pl.BlockSpec(
                    (tokens, size), lambda i, run: (0, jnp.minimum(run[0] * count + i, kept - 1))
                ),
                pl.BlockSpec(
                    (1, size, others),
                    lambda i, run: (jnp.clip(run[0] * count + i - kept, 0, again - 1), 0, 0),
                ),
                pl.BlockSpec((rows, size), lambda i, run: (0, run[0] * count + i)),
                column_half(tokens, width, 1),
                whole((rows, width)),
                whole((others, width)),
            ]
            + [ANY] * len(after),
            out_specs=pl.BlockSpec((size, width), lambda i, *_: (i, 0)),
        ),
        out_shape=jax.ShapeDtypeStruct((share, width), F32),
        compiler_params=params(),
        name="down_gradient_split",
        cost_estimate=cost(gathered, jax.ShapeDtypeStruct((share, width), F32)),
    )(run, mixed_all, act_rest, activated, gathered, own, rest, *after)


def held(values, after):
    count = len(values)
    return pl.pallas_call(
        lambda *refs: None,
        in_specs=[ANY] * (count + len(after)),
        out_specs=[ANY] * count,
        out_shape=[jax.ShapeDtypeStruct(v.shape, v.dtype) for v in values],
        input_output_aliases={k: k for k in range(count)},
        compiler_params=pltpu.CompilerParams(has_side_effects=True),
        name="held",
    )(*values, *after)


def body(inputs, out_grad, up_weight, mix_weight, output_factor_matrix, partner, local_perm):
    rows = inputs.shape[0]
    blocks, size = mix_weight.shape[1], mix_weight.shape[2]
    levels = partner.shape[0]
    up, down = up_weight[0], output_factor_matrix[0]
    width = up.shape[1]
    runs = lax.axis_size("dp")
    me, run = lax.axis_index("mp"), lax.axis_index("dp")
    base = me * blocks
    scale = (rows * runs) ** (-0.5)
    run_rows = ((run - jnp.arange(runs, dtype=jnp.int32)) % runs).astype(jnp.int32)
    perm_here = lax.dynamic_slice_in_dim(local_perm, base, blocks, 0) - base
    far_here = lax.dynamic_slice_in_dim(partner, base, blocks, 1)
    far_base = jnp.stack([jnp.bitwise_xor(me, 1 << lv) * blocks for lv in range(levels)])
    far_index = far_here - far_base[:, None]
    index = jnp.concatenate(
        [jnp.arange(blocks, dtype=jnp.int32)[None], perm_here[None], far_index], axis=0
    )
    which = [0, 0] + list(range(1, levels + 1))
    last = levels + 1
    part, share = size // runs, width // runs

    again = blocks // 3 if share % size == 0 else 0
    kept = blocks - again
    theirs = jnp.stack(
        [
            lax.dynamic_slice_in_dim(partner[lv], far_base[lv], blocks, 0) - base
            for lv in range(levels)
        ]
    )

    order = jnp.arange(blocks, dtype=jnp.int32)
    places = jnp.sum(
        jnp.where(theirs[:, None, :] == order[None, :, None], order[None, None, :], 0),
        axis=2,
        dtype=jnp.int32,
    )

    gathered = lax.all_gather(
        jnp.concatenate([inputs, out_grad], axis=1), "dp", axis=0, tiled=True
    )
    hidden = dense(inputs, up, BF16)
    received = [from_partner(hidden, "mp", lv) for lv in range(levels)]
    act_grad = dense(out_grad, down, F32, True, after=received[:-1])
    near = mixed_near(
        [hidden] + received[:-1], which[:-1], index[:-1], list(range(last)), mix_weight,
        after=(act_grad,),
    )
    mixed, activated, delta = mixed_last(
        received[-1], index[-1], last, mix_weight, near, act_grad, kept
    )
    mixed_all = lax.all_gather(mixed, "dp", axis=0, tiled=True)
    far = far_terms(delta, far_index, list(range(2, levels + 2)), mix_weight)
    far_received = [from_partner(far[lv], "mp", lv) for lv in range(levels)]
    outputs, act_grad_all = down_first(
        activated, down, inputs, gathered, kept * size, after=far[:1]
    )
    others, hidden_part, *sent = hidden_rows(
        up, gathered, run_rows, places, blocks, kept, part, rows,
        after=[outputs] + far_received[:1],
    )
    sources = [from_partner(piece, "mp", k % levels) for k, piece in enumerate(sent)]
    part_sources, whole_sources = sources[:levels], sources[levels:]
    run_next = ((run + jnp.arange(runs, dtype=jnp.int32)) % runs).astype(jnp.int32)
    hidden_grad, to_send = back_pass(
        delta, perm_here, mix_weight, far_received, run_next, after=[hidden_part] + sources[::levels]
    )
    rest = None
    if again:
        outputs, *rest = down_rest(
            activated, down, outputs, gathered, run_rows, kept * size, after=(hidden_grad,)
        )
    input_grad = dense_added(hidden_grad, up, out_grad, True, after=(outputs,))
    to_send = [to_send[0]] + list(held(to_send[1:], (input_grad, mixed_all)))
    hidden_grad_pieces = [to_send[0]] + [rotated(to_send[s], "dp", s) for s in range(1, runs)]
    made, act_rest = None, input_grad
    if again:
        made, act_rest = recomputed(
            [hidden, hidden] + received, delta, others, whole_sources, index, rest[0], run[None],
            mix_weight, scale, after=to_send[1:2],
        )
    if again:
        down_grad = down_gradient_split(
            mixed_all, act_rest, activated, gathered, out_grad, rest[1], run[None], share, scale,
        )
    else:
        down_grad = down_gradient(mixed_all, gathered, run, share, scale)
    mix_grad = mix_gradient(
        mixed_all, act_grad_all, hidden_part, part_sources, perm_here, scale, made,
        after=(down_grad,),
    )
    up_grad = up_gradient(
        gathered, up.shape[0], hidden_grad_pieces, run_rows, scale, after=(mix_grad,)
    )
    return (outputs, input_grad, up_grad[None], mix_grad, down_grad[None])


def solution(mesh):
    return jax.shard_map(
        body,
        mesh=mesh,
        in_specs=(
            P(("groups", "dp"), "mp"),
            P(("groups", "dp"), "mp"),
            P("mp", None, None),
            P(None, "mp", None, None),
            P("mp", None, None),
            P(),
            P(),
        ),
        out_specs=(
            P(("groups", "dp"), "mp"),
            P(("groups", "dp"), "mp"),
            P(("groups", "mp"), None, "dp"),
            P("groups", "mp", "dp", None),
            P(("groups", "mp"), "dp", None),
        ),
        check_vma=False,
    )
```

```python
import functools
import math

import jax
import jax.numpy as jnp
from jax import lax
from jax.experimental import pallas as pl
from jax.experimental.pallas import tpu as pltpu
from jax.sharding import PartitionSpec as P

F32 = jnp.float32
BF16 = jnp.bfloat16
VMEM_BYTES = 56 * 1024 * 1024
ANY = pl.BlockSpec(memory_space=pl.ANY)


def from_partner(value, axis, apart):
    mask = 2**apart
    pairs = [(source, source ^ mask) for source in range(lax.axis_size(axis))]
    return lax.ppermute(value, axis, pairs)


def rotated(value, axis, shift):
    size = lax.axis_size(axis)
    return lax.ppermute(value, axis, [(i, (i + shift) % size) for i in range(size)])


def gelu_tanh(values):
    inner = 0.7978845608028654 * (values + 0.044715 * values * values * values)
    return 0.5 * values * (1.0 + jnp.tanh(inner))


def gelu_slope(values):
    inner = 0.7978845608028654 * (values + 0.044715 * values * values * values)
    tangent = jnp.tanh(inner)
    return 0.5 * (1.0 + tangent) + 0.5 * values * (1.0 - tangent * tangent) * 0.7978845608028654 * (
        1.0 + 3.0 * 0.044715 * values * values
    )


def dot(a, b):
    return jnp.dot(a, b, preferred_element_type=F32)


def dot_nt(a, b):
    return lax.dot_general(a, b, (((1,), (1,)), ((), ())), preferred_element_type=F32)


def dot_tn(a, b):
    return lax.dot_general(a, b, (((0,), (0,)), ((), ())), preferred_element_type=F32)


def params():
    return pltpu.CompilerParams(vmem_limit_bytes=VMEM_BYTES)


def cost(*arrays):
    moved = sum(math.prod(a.shape) * a.dtype.itemsize for a in arrays)
    return pl.CostEstimate(flops=0, bytes_accessed=int(2.2 * moved), transcendentals=0)


def level_shape(mix_weight):
    return jax.ShapeDtypeStruct(mix_weight.shape[1:], mix_weight.dtype)


def chunk_of(block_count, most):
    return max(c for c in range(1, most + 1) if block_count % c == 0)


def lanes(index, size):
    return pl.ds(pl.multiple_of(index * size, size), size)


def whole(shape):
    return pl.BlockSpec(shape, lambda i, *_: (0,) * len(shape))


def column_half(tokens, features, half):
    return pl.BlockSpec((tokens, features), lambda i, *_: (0, half))


def weight_specs(levels, chunk, size):
    return [
        pl.BlockSpec((1, chunk, size, size), functools.partial(lambda lv, i, *_: (lv, i, 0, 0), lv))
        for lv in levels
    ]


def mixed_near(sources, which, index, levels, mix_weight, after=()):
    rows, width = sources[0].shape
    blocks, size = mix_weight.shape[1], mix_weight.shape[2]
    chunk = chunk_of(blocks, 8)
    count = len(levels)
    near_shape = jax.ShapeDtypeStruct((rows, width), F32)

    def kernel(index_ref, *refs):
        source_refs, weight_refs, out_ref = refs[: len(sources)], refs[len(sources) :], refs[-1]
        step = pl.program_id(0)
        for c in range(chunk):
            total = None
            for k in range(count):
                picked = source_refs[which[k]][:, lanes(index_ref[k, step * chunk + c], size)]
                term = dot(picked, weight_refs[k][0, c])
                total = term if total is None else total + term
            out_ref[:, c * size : (c + 1) * size] = total

    return pl.pallas_call(
        kernel,
        grid_spec=pltpu.PrefetchScalarGridSpec(
            num_scalar_prefetch=1,
            grid=(blocks // chunk,),
            in_specs=[whole((rows, width)) for _ in sources]
            + weight_specs(levels, chunk, size)
            + [ANY] * len(after),
            out_specs=pl.BlockSpec((rows, chunk * size), lambda i, *_: (0, i)),
        ),
        out_shape=near_shape,
        compiler_params=params(),
        name="mixed_near",
        cost_estimate=cost(*sources, *[level_shape(mix_weight)] * count, near_shape),
    )(index, *sources, *([mix_weight] * count), *after)


def mixed_last(source, index, level, mix_weight, near, act_grad, kept, after=()):
    rows, width = source.shape
    blocks, size = mix_weight.shape[1], mix_weight.shape[2]
    chunk = chunk_of(math.gcd(blocks, kept), 8)

    def kernel(index_ref, source_ref, weight_ref, near_ref, grad_ref, *refs):
        mixed_ref, act_ref, delta_ref = refs[-3:]
        step = pl.program_id(0)
        for c in range(chunk):
            here = slice(c * size, (c + 1) * size)
            picked = source_ref[:, lanes(index_ref[step * chunk + c], size)]
            total = near_ref[:, here] + dot(picked, weight_ref[0, c])

            @pl.when(step < kept // chunk)
            def _(total=total, here=here):
                mixed_ref[:, here] = total.astype(BF16)

            act_ref[:, here] = gelu_tanh(total).astype(BF16)
            delta_ref[:, here] = (grad_ref[:, here] * gelu_slope(total)).astype(BF16)

    columns = pl.BlockSpec((rows, chunk * size), lambda i, *_: (0, i))
    return pl.pallas_call(
        kernel,
        grid_spec=pltpu.PrefetchScalarGridSpec(
            num_scalar_prefetch=1,
            grid=(blocks // chunk,),
            in_specs=[whole((rows, width))] + weight_specs([level], chunk, size)
            + [columns, columns]
            + [ANY] * len(after),
            out_specs=[
                pl.BlockSpec((rows, chunk * size), lambda i, *_: (0, jnp.minimum(i, kept // chunk - 1))),
                columns,
                columns,
            ],
        ),
        out_shape=[jax.ShapeDtypeStruct((rows, kept * size), BF16)]
        + [jax.ShapeDtypeStruct((rows, width), BF16)] * 2,
        compiler_params=params(),
        name="mixed_last",
        cost_estimate=cost(source, level_shape(mix_weight), near, act_grad, source, source),
    )(index, source, mix_weight, near, act_grad, *after)


def far_terms(delta, targets, levels, mix_weight, after=()):
    rows, width = delta.shape
    blocks, size = mix_weight.shape[1], mix_weight.shape[2]
    chunk = chunk_of(blocks, 8)
    count = len(levels)

    def kernel(target_ref, delta_ref, *refs):
        step = pl.program_id(0)
        for c in range(chunk):
            here = delta_ref[:, c * size : (c + 1) * size]
            for k in range(count):
                place = lanes(target_ref[k, step * chunk + c], size)
                refs[count + len(after) + k][:, place] = dot_nt(here, refs[k][0, c]).astype(BF16)

    return pl.pallas_call(
        kernel,
        grid_spec=pltpu.PrefetchScalarGridSpec(
            num_scalar_prefetch=1,
            grid=(blocks // chunk,),
            in_specs=[pl.BlockSpec((rows, chunk * size), lambda i, *_: (0, i))]
            + weight_specs(levels, chunk, size)
            + [ANY] * len(after),
            out_specs=[whole((rows, width))] * count,
        ),
        out_shape=[jax.ShapeDtypeStruct((rows, width), BF16)] * count,
        compiler_params=params(),
        name="far_terms",
        cost_estimate=cost(delta, *[level_shape(mix_weight), delta] * count),
    )(targets, delta, *([mix_weight] * count), *after)


def back_pass(delta, perm, mix_weight, terms, run_next, after=()):
    rows, width = delta.shape
    blocks, size = mix_weight.shape[1], mix_weight.shape[2]
    chunk = chunk_of(blocks, 8)
    runs = run_next.shape[0]
    share = width // runs
    split = share % 128 == 0

    def kernel(perm_ref, run_ref, delta_ref, own_ref, perm_weight_ref, *refs):
        out_ref, *piece_refs, total_ref = refs[len(terms) + len(after) :]
        step = pl.program_id(0)

        @pl.when(step == 0)
        def _():
            total = refs[0][...].astype(F32)
            for term_ref in refs[1 : len(terms)]:
                total = total + term_ref[...].astype(F32)
            total_ref[...] = total

        for c in range(chunk):
            here = delta_ref[:, c * size : (c + 1) * size]
            total_ref[:, lanes(step * chunk + c, size)] += dot_nt(here, own_ref[0, c])
            total_ref[:, lanes(perm_ref[step * chunk + c], size)] += dot_nt(here, perm_weight_ref[0, c])

        @pl.when(step == blocks // chunk - 1)
        def _():
            out_ref[...] = total_ref[...].astype(BF16)
            for s, piece_ref in enumerate(piece_refs):
                piece_ref[...] = total_ref[:, lanes(run_ref[s], share)].astype(BF16)

    results = pl.pallas_call(
        kernel,
        grid_spec=pltpu.PrefetchScalarGridSpec(
            num_scalar_prefetch=2,
            grid=(blocks // chunk,),
            in_specs=[pl.BlockSpec((rows, chunk * size), lambda i, *_: (0, i))]
            + weight_specs([0, 1], chunk, size)
            + [whole((rows, width))] * len(terms)
            + [ANY] * len(after),
            out_specs=[whole((rows, width))] + [whole((rows, share))] * (runs if split else 0),
            scratch_shapes=[pltpu.VMEM((rows, width), F32)],
        ),
        out_shape=[jax.ShapeDtypeStruct((rows, width), BF16)]
        + [jax.ShapeDtypeStruct((rows, share), BF16)] * (runs if split else 0),
        compiler_params=params(),
        name="back_pass",
        cost_estimate=cost(delta, *terms, *[level_shape(mix_weight)] * 2),
    )(perm, run_next, delta, mix_weight, mix_weight, *terms, *after)
    if split:
        return results[0], results[1:]
    return results[0], [
        lax.dynamic_slice_in_dim(results[0], run_next[s] * share, share, 1) for s in range(runs)
    ]


def dense(left, right, out_type, right_transposed=False, after=()):
    rows, depth = left.shape
    width = right.shape[0] if right_transposed else right.shape[1]
    step = chunk_of(width // 128, 12) * 128
    out_shape = jax.ShapeDtypeStruct((rows, width), out_type)
    if right_transposed:
        right_spec = pl.BlockSpec((step, depth), lambda i: (i, 0))
    else:
        right_spec = pl.BlockSpec((depth, step), lambda i: (0, i))

    def kernel(left_ref, right_ref, *refs):
        product = (dot_nt if right_transposed else dot)(left_ref[...], right_ref[...])
        refs[-1][...] = product.astype(out_type)

    return pl.pallas_call(
        kernel,
        grid=(width // step,),
        in_specs=[whole((rows, depth)), right_spec] + [ANY] * len(after),
        out_specs=pl.BlockSpec((rows, step), lambda i: (0, i)),
        out_shape=out_shape,
        compiler_params=params(),
        name="dense_nt" if right_transposed else "dense",
        cost_estimate=cost(left, right, out_shape),
    )(left, right, *after)


def dense_added(left, right, base, right_transposed=False, after=()):
    rows, depth = left.shape
    width = base.shape[1]
    step = chunk_of(depth // 128, 12) * 128
    if right_transposed:
        right_spec = pl.BlockSpec((width, step), lambda i: (0, i))
    else:
        right_spec = pl.BlockSpec((step, width), lambda i: (i, 0))

    def kernel(left_ref, right_ref, base_ref, *refs):
        out_ref, total_ref = refs[-2], refs[-1]
        here = pl.program_id(0)

        @pl.when(here == 0)
        def _():
            total_ref[...] = base_ref[...].astype(F32)

        total_ref[...] += (dot_nt if right_transposed else dot)(left_ref[...], right_ref[...])

        @pl.when(here == depth // step - 1)
        def _():
            out_ref[...] = total_ref[...].astype(out_ref.dtype)

    return pl.pallas_call(
        kernel,
        grid=(depth // step,),
        in_specs=[pl.BlockSpec((rows, step), lambda i: (0, i)), right_spec, whole(base.shape)]
        + [ANY] * len(after),
        out_specs=whole(base.shape),
        out_shape=jax.ShapeDtypeStruct(base.shape, base.dtype),
        scratch_shapes=[pltpu.VMEM(base.shape, F32)],
        compiler_params=params(),
        name="added_nt" if right_transposed else "added",
        cost_estimate=cost(left, right, base),
    )(left, right, base, *after)


def hidden_rows(up, gathered, run_rows, places, blocks, kept, part, rows, after=()):
    depth, width = up.shape
    tokens = gathered.shape[0]
    size = width // blocks
    chunk = chunk_of(blocks, 6)
    levels = places.shape[0]
    again = blocks - kept
    others = tokens - rows
    sent = [jax.ShapeDtypeStruct((kept * part, tokens), BF16)] * levels
    if again:
        sent += [jax.ShapeDtypeStruct((again * size, others), BF16)] * levels

    def kernel(run_ref, place_ref, up_ref, inputs_ref, *refs):
        whole_ref, out_ref, *sent_refs, full_ref = refs[len(after) :]
        full_ref[...] = dot(inputs_ref[...], up_ref[...]).astype(BF16).T
        for c in range(chunk):
            first = pl.multiple_of(run_ref[0] * part, part) + c * size
            for s in range(1, tokens // rows):
                there = pl.multiple_of(run_ref[s] * rows, rows)
                piece = full_ref[c * size : (c + 1) * size, pl.ds(there, rows)]
                whole_ref[c, :, (s - 1) * rows : s * rows] = piece
            out_ref[c] = full_ref[pl.ds(first, part), :]
            for lv in range(levels):
                place = place_ref[lv, pl.program_id(0) * chunk + c]

                if again:

                    @pl.when(place >= kept)
                    def _(place=place, lv=lv, c=c):
                        there = pl.multiple_of((place - kept) * size, size)
                        sent_refs[levels + lv][pl.ds(there, size), :] = whole_ref[c]

                @pl.when(place < kept)
                def _(place=place, lv=lv, c=c):
                    there = pl.multiple_of(place * part, part)
                    sent_refs[lv][pl.ds(there, part), :] = out_ref[c]

    return pl.pallas_call(
        kernel,
        grid_spec=pltpu.PrefetchScalarGridSpec(
            num_scalar_prefetch=2,
            grid=(blocks // chunk,),
            in_specs=[
                pl.BlockSpec((depth, chunk * size), lambda i, *_: (0, i)),
                column_half(tokens, depth, 0),
            ]
            + [ANY] * len(after),
            out_specs=[
                pl.BlockSpec((chunk, size, others), lambda i, *_: (i, 0, 0)),
                pl.BlockSpec((chunk, part, tokens), lambda i, *_: (i, 0, 0)),
            ]
            + [whole(shape.shape) for shape in sent],
            scratch_shapes=[pltpu.VMEM((chunk * size, tokens), BF16)],
        ),
        out_shape=[
            jax.ShapeDtypeStruct((blocks, size, others), BF16),
            jax.ShapeDtypeStruct((blocks, part, tokens), BF16),
        ]
        + sent,
        compiler_params=params(),
        name="hidden_rows",
        cost_estimate=cost(up, jax.ShapeDtypeStruct((blocks, size, tokens), BF16)),
    )(run_rows, places, up, gathered, *after)


def down_first(activated, down, base, gathered, kept, after=()):
    rows, width = activated.shape
    features = down.shape[1]
    tokens = gathered.shape[0]
    step = chunk_of(math.gcd(width, kept) // 128, 8) * 128
    out_type = BF16 if kept == width else F32

    def kernel(act_ref, down_ref, base_ref, all_ref, *refs):
        out_ref, grad_ref, total_ref = refs[-3:]
        here = pl.program_id(0)

        @pl.when(here == 0)
        def _():
            total_ref[...] = base_ref[...].astype(F32)

        total_ref[...] += dot(act_ref[...], down_ref[...])
        grad_ref[...] = dot_nt(all_ref[...], down_ref[...]).astype(BF16)

        @pl.when(here == kept // step - 1)
        def _():
            out_ref[...] = total_ref[...].astype(out_type)

    out_shape = [
        jax.ShapeDtypeStruct((rows, features), out_type),
        jax.ShapeDtypeStruct((tokens, kept), BF16),
    ]
    return pl.pallas_call(
        kernel,
        grid=(kept // step,),
        in_specs=[
            pl.BlockSpec((rows, step), lambda i: (0, i)),
            pl.BlockSpec((step, features), lambda i: (i, 0)),
            whole((rows, features)),
            column_half(tokens, features, 1),
        ]
        + [ANY] * len(after),
        out_specs=[
            whole((rows, features)),
            pl.BlockSpec((tokens, step), lambda i: (0, i)),
        ],
        out_shape=out_shape,
        scratch_shapes=[pltpu.VMEM((rows, features), F32)],
        compiler_params=params(),
        name="down_first",
        cost_estimate=cost(activated, down, out_shape[1]),
    )(activated, down, base, gathered, *after)


def down_rest(activated, down, partial, gathered, run_rows, kept, after=()):
    rows, width = activated.shape
    features = down.shape[1]
    tokens = gathered.shape[0]
    others = tokens - rows
    step = chunk_of(math.gcd(width, kept) // 128, 8) * 128
    first = kept // step

    def kernel(run_ref, act_ref, down_ref, partial_ref, all_ref, *refs):
        out_ref, grad_ref, rest_ref, total_ref = refs[-4:]
        here = pl.program_id(0)

        @pl.when(here == 0)
        def _():
            total_ref[...] = partial_ref[...]
            for s in range(1, tokens // rows):
                there = pl.multiple_of(run_ref[s] * rows, rows)
                rest_ref[(s - 1) * rows : s * rows, :] = all_ref[pl.ds(there, rows), :]

        total_ref[...] += dot(act_ref[...], down_ref[...])
        grad_ref[...] = dot_nt(down_ref[...], rest_ref[...])

        @pl.when(here == width // step - first - 1)
        def _():
            out_ref[...] = total_ref[...].astype(BF16)

    out_shape = [
        jax.ShapeDtypeStruct((rows, features), BF16),
        jax.ShapeDtypeStruct((width - kept, others), F32),
        jax.ShapeDtypeStruct((others, features), BF16),
    ]
    return pl.pallas_call(
        kernel,
        grid_spec=pltpu.PrefetchScalarGridSpec(
            num_scalar_prefetch=1,
            grid=(width // step - first,),
            in_specs=[
                pl.BlockSpec((rows, step), lambda i, *_: (0, first + i)),
                pl.BlockSpec((step, features), lambda i, *_: (first + i, 0)),
                whole((rows, features)),
                column_half(tokens, features, 1),
            ]
            + [ANY] * len(after),
            out_specs=[
                whole((rows, features)),
                pl.BlockSpec((step, others), lambda i, *_: (i, 0)),
                whole((others, features)),
            ],
            scratch_shapes=[pltpu.VMEM((rows, features), F32)],
        ),
        out_shape=out_shape,
        compiler_params=params(),
        name="down_rest",
        cost_estimate=cost(out_shape[1], out_shape[1], partial, partial),
    )(run_rows, activated, down, partial, gathered, *after)


def mix_gradient(mixed_all, act_grad_all, hidden_part, received, perm, scale, made=None, after=()):
    tokens, width = mixed_all.shape
    blocks, part, _ = hidden_part.shape
    size = part * lax.axis_size("dp")
    kept = width // size
    chunk = chunk_of(kept, 4)
    count = 2 + len(received)
    given = pl.BlockSpec((chunk * part, tokens), lambda i, *_: (i, 0))

    def kernel(perm_ref, mixed_ref, grad_ref, part_ref, *refs):
        given_refs, out_ref = refs[: len(received)], refs[-1]
        step = pl.program_id(0)
        for c in range(chunk):
            here = slice(c * size, (c + 1) * size)
            block = step * chunk + c
            slope = gelu_slope(mixed_ref[:, here].astype(F32))
            delta = (grad_ref[:, here].astype(F32) * slope).astype(BF16)
            rows = slice(c * part, (c + 1) * part)
            picked = jnp.concatenate(
                [part_ref[block], part_ref[perm_ref[block]]] + [ref[rows, :] for ref in given_refs],
                axis=0,
            )
            result = dot(picked, delta) * scale
            for k in range(count):
                out_ref[k, c] = result[k * part : (k + 1) * part]

    columns = pl.BlockSpec((tokens, chunk * size), lambda i, *_: (0, i))
    return pl.pallas_call(
        kernel,
        grid_spec=pltpu.PrefetchScalarGridSpec(
            num_scalar_prefetch=1,
            grid=(kept // chunk,),
            in_specs=[columns, columns, whole(hidden_part.shape)]
            + [given] * len(received)
            + ([] if made is None else [ANY])
            + [ANY] * len(after),
            out_specs=pl.BlockSpec((count, chunk, part, size), lambda i, *_: (0, i, 0, 0)),
        ),
        out_shape=jax.ShapeDtypeStruct((count, blocks, part, size), F32),
        input_output_aliases={} if made is None else {4 + len(received): 0},
        compiler_params=params(),
        name="mix_gradient",
        cost_estimate=cost(mixed_all, act_grad_all),
    )(perm, mixed_all, act_grad_all, hidden_part, *received, *([] if made is None else [made]), *after)


def recomputed(
    own_sources, own_delta, others, received, index, act_grad_rest, run, mix_weight, scale, after=()
):
    blocks, size, tokens = others.shape
    rows = own_delta.shape[0]
    count = mix_weight.shape[0]
    again = act_grad_rest.shape[0] // size
    kept = blocks - again
    part = size // lax.axis_size("dp")
    chunk = chunk_of(math.gcd(again, kept), 2)

    def kernel(index_ref, run_ref, *refs):
        straight_ref, *refs = refs
        permuted_refs, refs = refs[:chunk], refs[chunk:]
        received_refs, refs = refs[: len(received)], refs[len(received) :]
        own_refs, refs = refs[: count * chunk], refs[count * chunk :]
        weight_refs, refs = refs[:count], refs[count:]
        grad_ref, delta_ref = refs[:2]
        out_ref, act_ref, full_ref = refs[-3:]
        first = pl.multiple_of(run_ref[0] * part, part)
        for c in range(chunk):
            here = pl.ds(c * size, size)
            sources = [straight_ref.at[c], permuted_refs[c].at[0]]
            sources += [ref.at[here] for ref in received_refs]
            mixed = None
            for k in range(count):
                term = dot_tn(weight_refs[k][0, c], sources[k][...])
                mixed = term if mixed is None else mixed + term
                full_ref[c * count + k] = dot_tn(own_refs[k * chunk + c][...], delta_ref[:, here])
            act_ref[c] = gelu_tanh(mixed).astype(BF16)
            delta = (grad_ref[here, :] * gelu_slope(mixed)).astype(BF16)
            picked = jnp.concatenate([ref[pl.ds(first, part), :] for ref in sources], axis=0)
            result = dot_nt(picked, delta)
            for k in range(count):
                own = full_ref[c * count + k, pl.ds(first, part), :]
                out_ref[k, c] = (result[k * part : (k + 1) * part] + own) * scale

    source_specs = [
        pl.BlockSpec((chunk, size, tokens), lambda i, *_: (kept // chunk + i, 0, 0))
    ]
    for c in range(chunk):
        source_specs.append(
            pl.BlockSpec(
                (1, size, tokens),
                functools.partial(lambda c, i, index, run: (index[1, kept + i * chunk + c], 0, 0), c),
            )
        )
    source_specs += [pl.BlockSpec((chunk * size, tokens), lambda i, *_: (i, 0))] * len(received)
    own_specs = [
        pl.BlockSpec(
            (rows, size),
            functools.partial(
                lambda k, c, i, index, run: (0, index[k, kept + i * chunk + c]), k, c
            ),
        )
        for k in range(count)
        for c in range(chunk)
    ]
    level_specs = [
        pl.BlockSpec(
            (1, chunk, size, size),
            functools.partial(lambda k, i, *_: (k, kept // chunk + i, 0, 0), k),
        )
        for k in range(count)
    ]
    return pl.pallas_call(
        kernel,
        grid_spec=pltpu.PrefetchScalarGridSpec(
            num_scalar_prefetch=2,
            grid=(again // chunk,),
            in_specs=source_specs
            + own_specs
            + level_specs
            + [
                pl.BlockSpec((chunk * size, tokens), lambda i, *_: (i, 0)),
                pl.BlockSpec((rows, chunk * size), lambda i, *_: (0, kept // chunk + i)),
            ]
            + [ANY] * len(after),
            out_specs=[
                pl.BlockSpec((count, chunk, part, size), lambda i, *_: (0, kept // chunk + i, 0, 0)),
                pl.BlockSpec((chunk, size, tokens), lambda i, *_: (i, 0, 0)),
            ],
            scratch_shapes=[pltpu.VMEM((chunk * count, size, size), F32)],
        ),
        out_shape=[
            jax.ShapeDtypeStruct((count, blocks, part, size), F32),
            jax.ShapeDtypeStruct((again, size, tokens), BF16),
        ],
        compiler_params=params(),
        name="recomputed",
        cost_estimate=cost(*received, *received, act_grad_rest),
    )(
        index, run, others, *([others] * chunk), *received,
        *[source for source in own_sources for _ in range(chunk)], *([mix_weight] * count),
        act_grad_rest, own_delta, *after,
    )


def up_gradient(gathered, height, pieces, run_rows, scale, after=()):
    tokens = gathered.shape[0]
    rows, width = pieces[0].shape
    runs = len(pieces)
    step = chunk_of(height // 128, 4) * 128

    def kernel(run_ref, inputs_ref, *refs):
        out_ref, all_ref = refs[-2:]

        @pl.when(pl.program_id(0) == 0)
        def _():
            for s in range(runs):
                first = pl.multiple_of(run_ref[s] * rows, rows)
                all_ref[pl.ds(first, rows), :] = refs[s][...]

        out_ref[...] = dot_tn(inputs_ref[...], all_ref[...]) * scale

    return pl.pallas_call(
        kernel,
        grid_spec=pltpu.PrefetchScalarGridSpec(
            num_scalar_prefetch=1,
            grid=(height // step,),
            in_specs=[pl.BlockSpec((tokens, step), lambda i, *_: (0, i))]
            + [whole((rows, width))] * runs
            + [ANY] * len(after),
            out_specs=pl.BlockSpec((step, width), lambda i, *_: (i, 0)),
            scratch_shapes=[pltpu.VMEM((tokens, width), BF16)],
        ),
        out_shape=jax.ShapeDtypeStruct((height, width), F32),
        compiler_params=params(),
        name="up_gradient",
        cost_estimate=cost(gathered, jax.ShapeDtypeStruct((height, width), F32)),
    )(run_rows, gathered, *pieces, *after)


def down_gradient(mixed_all, gathered, run, share, scale, after=()):
    tokens, width = gathered.shape[0], gathered.shape[1] // 2
    if share % 128 == 0:
        step = chunk_of(share // 128, 4) * 128
        first = run * (share // step)
    else:
        mixed_all = lax.dynamic_slice_in_dim(mixed_all, run * share, share, 1)
        step, first = share, run * 0

    def kernel(first_ref, mixed_ref, right_ref, *refs):
        activated = gelu_tanh(mixed_ref[...].astype(F32)).astype(BF16)
        refs[-1][...] = dot_tn(activated, right_ref[...]) * scale

    return pl.pallas_call(
        kernel,
        grid_spec=pltpu.PrefetchScalarGridSpec(
            num_scalar_prefetch=1,
            grid=(share // step,),
            in_specs=[
                pl.BlockSpec((tokens, step), lambda i, first: (0, first[0] + i)),
                column_half(tokens, width, 1),
            ]
            + [ANY] * len(after),
            out_specs=pl.BlockSpec((step, width), lambda i, *_: (i, 0)),
        ),
        out_shape=jax.ShapeDtypeStruct((share, width), F32),
        compiler_params=params(),
        name="down_gradient",
        cost_estimate=cost(gathered, jax.ShapeDtypeStruct((share, width), F32)),
    )(first[None], mixed_all, gathered, *after)


def down_gradient_split(
    mixed_all, act_rest, activated, gathered, own, rest, run, share, scale, after=()
):
    tokens, width = gathered.shape[0], gathered.shape[1] // 2
    again, size, others = act_rest.shape
    rows, kept = activated.shape[0], mixed_all.shape[1] // size
    count = share // size

    def kernel(run_ref, mixed_ref, act_ref, own_act_ref, right_ref, own_ref, rest_ref, *refs):
        out_ref = refs[-1]
        block = run_ref[0] * count + pl.program_id(0)

        @pl.when(block < kept)
        def _():
            act = gelu_tanh(mixed_ref[...].astype(F32)).astype(BF16)
            out_ref[...] = dot_tn(act, right_ref[...]) * scale

        @pl.when(block >= kept)
        def _():
            total = dot(act_ref[0], rest_ref[...]) + dot_tn(own_act_ref[...], own_ref[...])
            out_ref[...] = total * scale

    return pl.pallas_call(
        kernel,
        grid_spec=pltpu.PrefetchScalarGridSpec(
            num_scalar_prefetch=1,
            grid=(count,),
            in_specs=[
                pl.BlockSpec(
                    (tokens, size), lambda i, run: (0, jnp.minimum(run[0] * count + i, kept - 1))
                ),
                pl.BlockSpec(
                    (1, size, others),
                    lambda i, run: (jnp.clip(run[0] * count + i - kept, 0, again - 1), 0, 0),
                ),
                pl.BlockSpec((rows, size), lambda i, run: (0, run[0] * count + i)),
                column_half(tokens, width, 1),
                whole((rows, width)),
                whole((others, width)),
            ]
            + [ANY] * len(after),
            out_specs=pl.BlockSpec((size, width), lambda i, *_: (i, 0)),
        ),
        out_shape=jax.ShapeDtypeStruct((share, width), F32),
        compiler_params=params(),
        name="down_gradient_split",
        cost_estimate=cost(gathered, jax.ShapeDtypeStruct((share, width), F32)),
    )(run, mixed_all, act_rest, activated, gathered, own, rest, *after)


def held(values, after):
    count = len(values)
    return pl.pallas_call(
        lambda *refs: None,
        in_specs=[ANY] * (count + len(after)),
        out_specs=[ANY] * count,
        out_shape=[jax.ShapeDtypeStruct(v.shape, v.dtype) for v in values],
        input_output_aliases={k: k for k in range(count)},
        compiler_params=pltpu.CompilerParams(has_side_effects=True),
        name="held",
    )(*values, *after)


def body(inputs, out_grad, up_weight, mix_weight, output_factor_matrix, partner, local_perm):
    rows = inputs.shape[0]
    blocks, size = mix_weight.shape[1], mix_weight.shape[2]
    levels = partner.shape[0]
    up, down = up_weight[0], output_factor_matrix[0]
    width = up.shape[1]
    runs = lax.axis_size("dp")
    me, run = lax.axis_index("mp"), lax.axis_index("dp")
    base = me * blocks
    scale = (rows * runs) ** (-0.5)
    run_rows = ((run - jnp.arange(runs, dtype=jnp.int32)) % runs).astype(jnp.int32)
    perm_here = lax.dynamic_slice_in_dim(local_perm, base, blocks, 0) - base
    far_here = lax.dynamic_slice_in_dim(partner, base, blocks, 1)
    far_base = jnp.stack([jnp.bitwise_xor(me, 1 << lv) * blocks for lv in range(levels)])
    far_index = far_here - far_base[:, None]
    index = jnp.concatenate(
        [jnp.arange(blocks, dtype=jnp.int32)[None], perm_here[None], far_index], axis=0
    )
    which = [0, 0] + list(range(1, levels + 1))
    last = levels + 1
    part, share = size // runs, width // runs

    again = blocks // 3 if share % size == 0 else 0
    kept = blocks - again
    theirs = jnp.stack(
        [
            lax.dynamic_slice_in_dim(partner[lv], far_base[lv], blocks, 0) - base
            for lv in range(levels)
        ]
    )

    order = jnp.arange(blocks, dtype=jnp.int32)
    places = jnp.sum(
        jnp.where(theirs[:, None, :] == order[None, :, None], order[None, None, :], 0),
        axis=2,
        dtype=jnp.int32,
    )

    gathered = lax.all_gather(
        jnp.concatenate([inputs, out_grad], axis=1), "dp", axis=0, tiled=True
    )
    hidden = dense(inputs, up, BF16)
    received = [from_partner(hidden, "mp", lv) for lv in range(levels)]
    act_grad = dense(out_grad, down, F32, True, after=received[:-1])
    near = mixed_near(
        [hidden] + received[:-1], which[:-1], index[:-1], list(range(last)), mix_weight,
        after=(act_grad,),
    )
    mixed, activated, delta = mixed_last(
        received[-1], index[-1], last, mix_weight, near, act_grad, kept
    )
    mixed_all = lax.all_gather(mixed, "dp", axis=0, tiled=True)
    far = far_terms(delta, far_index, list(range(2, levels + 2)), mix_weight)
    far_received = [from_partner(far[lv], "mp", lv) for lv in range(levels)]
    outputs, act_grad_all = down_first(
        activated, down, inputs, gathered, kept * size, after=far[:1]
    )
    others, hidden_part, *sent = hidden_rows(
        up, gathered, run_rows, places, blocks, kept, part, rows,
        after=[outputs] + far_received[:1],
    )
    sources = [from_partner(piece, "mp", k % levels) for k, piece in enumerate(sent)]
    part_sources, whole_sources = sources[:levels], sources[levels:]
    run_next = ((run + jnp.arange(runs, dtype=jnp.int32)) % runs).astype(jnp.int32)
    hidden_grad, to_send = back_pass(
        delta, perm_here, mix_weight, far_received, run_next, after=[hidden_part] + sources[::levels]
    )
    rest = None
    if again:
        outputs, *rest = down_rest(
            activated, down, outputs, gathered, run_rows, kept * size, after=(hidden_grad,)
        )
    input_grad = dense_added(hidden_grad, up, out_grad, True, after=(outputs,))
    to_send = [to_send[0]] + list(held(to_send[1:], (input_grad, mixed_all)))
    hidden_grad_pieces = [to_send[0]] + [rotated(to_send[s], "dp", s) for s in range(1, runs)]
    made, act_rest = None, input_grad
    if again:
        made, act_rest = recomputed(
            [hidden, hidden] + received, delta, others, whole_sources, index, rest[0], run[None],
            mix_weight, scale, after=to_send[1:2],
        )
    if again:
        down_grad = down_gradient_split(
            mixed_all, act_rest, activated, gathered, out_grad, rest[1], run[None], share, scale,
        )
    else:
        down_grad = down_gradient(mixed_all, gathered, run, share, scale)
    mix_grad = mix_gradient(
        mixed_all, act_grad_all, hidden_part, part_sources, perm_here, scale, made,
        after=(down_grad,),
    )
    up_grad = up_gradient(
        gathered, up.shape[0], hidden_grad_pieces, run_rows, scale, after=(mix_grad,)
    )
    return (outputs, input_grad, up_grad[None], mix_grad, down_grad[None])


def solution(mesh):
    return jax.shard_map(
        body,
        mesh=mesh,
        in_specs=(
            P(("groups", "dp"), "mp"),
            P(("groups", "dp"), "mp"),
            P("mp", None, None),
            P(None, "mp", None, None),
            P("mp", None, None),
            P(),
            P(),
        ),
        out_specs=(
            P(("groups", "dp"), "mp"),
            P(("groups", "dp"), "mp"),
            P(("groups", "mp"), None, "dp"),
            P("groups", "mp", "dp", None),
            P(("groups", "mp"), "dp", None),
        ),
        check_vma=False,
    )
```
